128 devices in a mesh: dp: 4 (over z), tensor: 32 (over x, y, core).
Axes of the slice: x: 4, y: 4, z: 4, core: 2. Of those that a mesh axis runs over, the one named last changes fastest.
Arguments:
- x_rows: bfloat16 [16384, 4096], P(('dp', 'tensor')), may hold values from -6 to 6
- grad_out: bfloat16 [16384, 16384], P('dp', 'tensor'), may hold values from -0.0625 to 0.0625
- error_buffer: float32 [4, 4096, 16384], P('dp', None, 'tensor'), may hold values from -12 to 12, as said below
- q_init: float32 [16384, 32], P('tensor'), may hold values from -6 to 6
Outputs:
- new_error: float32 [4, 4096, 16384], P('dp', None, 'tensor')
- p_basis: float32 [4096, 32], replicated
- q_factor: float32 [16384, 32], P('tensor')
The draws below stay inside these ranges and needn't reach their ends.
Inputs may be any that keep to these rules, and one draw needn't show every extreme that they name: `error_buffer`: finite float32 values.
All inputs are finite; a program needn't handle non-finite values.
Results may differ from the reference program's by a relative error of at most 0.0003.
Values may be sent and summed in bfloat16 or wider, within the bound.
No kernel may reach another device: no remote copies, remote signals or barrier semaphores. Data moves between devices by JAX's collectives and lax.ppermute only.
A program may use at most 128 MiB of HBM per device.

```python
import math
import jax
import jax.numpy as jnp
from jax import lax

D = 4096
FF = 16384
R = 32
TOK_DEV = 128
TOK_R = 4096
TOKENS = 16384
N_DP = 4
N_TENSOR = 32


def draw_error_buffer(key, part):
    key = jax.random.fold_in(key, 7)
    key_rows, key_cols, key_own = jax.random.split(key, 3)
    row_scale = jnp.exp(jax.random.uniform(key_rows, (D,), jnp.float32) * math.log(10.0))
    row_scale = row_scale * jnp.power(3.0, jnp.arange(D, dtype=jnp.float32) / D)
    col_scale = jnp.exp(jax.random.uniform(key_cols, (FF,), jnp.float32) * math.log(10.0))
    base_values = jax.random.normal(key_own, (N_DP, D, FF), jnp.float32)
    base_values = jnp.clip(base_values, -4.0, 4.0)
    return (base_values * row_scale[None, :, None] * col_scale[None, None, :] * 0.01).astype(jnp.float32)


def level_of(key, extent, cuts, least, largest):
    level, own = 1.0, jax.random.fold_in(key, 6)
    for dim, shards_of in cuts:
        heights = jnp.exp(jax.random.uniform(jax.random.fold_in(own, dim), (shards_of,), jnp.float32, least / len(cuts), largest / len(cuts)))
        level = level * jnp.repeat(heights, extent[dim] // shards_of).reshape([-1 if axis == dim else 1 for axis in range(len(extent))])
    return level


def noise(stream_key, extent, deviation, most, shards=(), kind=jnp.bfloat16):
    result = deviation * jax.random.normal(stream_key, extent, jnp.float32)
    if shards:
        result = result * level_of(stream_key, extent, shards, -0.22, 0.18)
    return jnp.clip(result, -most, most).astype(kind)


def setup_inputs(seed: int = 0) -> dict:
    keys = jax.random.split(jax.random.key(seed), 5)
    return {
        "x_rows": noise(keys[0], (TOKENS, D), 1.0, 6.0, ((0, 128),)),
        "grad_out": noise(keys[1], (TOKENS, FF), (0.3 * (TOK_DEV * N_TENSOR) ** -0.5), 0.0625, ((0, 4), (1, 32))),
        "error_buffer": draw_error_buffer(jax.random.fold_in(keys[4], 71), 0),
        "q_init": noise(keys[3], (FF, R), 1.0, 6.0, ((0, 32),), jnp.float32),
    }


def reference(x_rows, grad_out, error_buffer, q_init):
    merged_all = []
    for replica in range(N_DP):
        x_part = x_rows[replica * TOK_R:(replica + 1) * TOK_R]
        out_part = grad_out[replica * TOK_R:(replica + 1) * TOK_R]
        gradient = jnp.dot(x_part.T.astype(jnp.float32), out_part.astype(jnp.float32), preferred_element_type=jnp.float32)
        merged_all.append(error_buffer[replica] + gradient)
    sketch = jnp.zeros((D, R), jnp.float32)
    for replica in range(N_DP):
        sketch = sketch + jnp.dot(merged_all[replica], q_init, precision=lax.Precision.HIGHEST)
    sketch = sketch / N_DP
    gram_matrix = jnp.dot(sketch.T, sketch, precision=lax.Precision.HIGHEST)
    lower_factor = jnp.linalg.cholesky(gram_matrix)
    p_basis = lax.linalg.triangular_solve(lower_factor, sketch, left_side=False, lower=True, transpose_a=True)
    q_factor = jnp.zeros((FF, R), jnp.float32)
    for replica in range(N_DP):
        q_factor = q_factor + jnp.dot(merged_all[replica].T, p_basis, precision=lax.Precision.HIGHEST)
    q_factor = q_factor / N_DP
    approx = jnp.dot(p_basis, q_factor.T, precision=lax.Precision.HIGHEST)
    new_error = jnp.stack([merged_all[replica] - approx for replica in range(N_DP)])
    return (new_error, p_basis, q_factor)
```

```python
import functools

import jax
import jax.numpy as jnp
import numpy as np
from jax import lax
from jax.experimental import pallas as pl
from jax.experimental.pallas import tpu as pltpu
from jax.sharding import PartitionSpec as P

F32, BF16 = jnp.float32, jnp.bfloat16
N, R, D, F, T = 4, 32, 4096, 512, 128
OFFSETS = (0, -1, 1, 2)
VMEM_LIMIT = 56 * 1024 * 1024
WHOLE = pl.BlockSpec(memory_space=pltpu.VMEM)
SMEM = pl.BlockSpec(memory_space=pltpu.SMEM)
NT = (((1,), (1,)), ((), ()))
TN = (((0,), (0,)), ((), ()))


def flat(x, y, c):
    return ((x % N) * N + y % N) * 2 + c


def along(x, y, c, first, d):
    return flat(x + d, y, c) if (c == 0) == first else flat(x, y + d, c)


PLANE = [(x, y, c) for x in range(N) for y in range(N) for c in range(2)]


def hop(array, first, d):
    pairs = [(flat(*p), along(*p, first, d)) for p in PLANE]
    return lax.ppermute(array, "tensor", pairs)


def swap(array):
    return lax.ppermute(array, "tensor", [(i, i ^ 1) for i in range(2 * N * N)])


def hop_z(array, d):
    return lax.ppermute(array, "dp", [(i, (i + d) % N) for i in range(N)])


def block_table():
    table = np.zeros((2 * N * N, 2, N, N), np.int32)
    for x, y, c in PLANE:
        for k in range(2):
            colour = c ^ k
            for i, second in enumerate(OFFSETS):
                for j, first in enumerate(OFFSETS):
                    dx, dy = (first, second) if colour == 0 else (second, first)
                    table[flat(x, y, c), k, i, j] = flat(x + dx, y + dy, colour) * T
    return table.reshape(2 * N * N, 2 * N * N)


def split(value, parts):
    pieces = []
    for _ in range(parts):
        piece = value.astype(BF16)
        pieces.append(piece)
        value = value - piece.astype(F32)
    return pieces


def dot(a, b, dims=(((1,), (0,)), ((), ()))):
    return lax.dot_general(a, b, dims, preferred_element_type=F32)


def dot_left(value, exact, dims):
    rows = value.shape[0]
    out = dot(jnp.concatenate(split(value, 3), 0), exact, dims)
    return out[:rows] + (out[rows : 2 * rows] + out[2 * rows :])


def dot_both(value, other, dims):
    rows = value.shape[0]
    a = jnp.concatenate(split(value, 3), 0)
    b1, b2, b3 = split(other, 3)
    p1, p2, p3 = dot(a, b1, dims), dot(a[: 2 * rows], b2, dims), dot(a[:rows], b3, dims)
    low = p1[2 * rows :] + p2[rows:] + p3
    return p1[:rows] + ((p1[rows : 2 * rows] + p2[:rows]) + low)


def params(**kw):
    return pltpu.CompilerParams(vmem_limit_bytes=VMEM_LIMIT, **kw)


def cost(flops, nbytes):
    return pl.CostEstimate(flops=int(flops), bytes_accessed=int(nbytes), transcendentals=0)


def shape(dims, dtype=F32):
    return jax.ShapeDtypeStruct(dims, dtype)


def tokens_kernel(off_ref, q_ref, g_ref, own_ref, other_ref):
    q = jnp.concatenate(split(q_ref[...], 3), 0)
    for k, out in enumerate((own_ref, other_ref)):
        for i in range(N):
            rows = []
            for j in range(N):
                at = pl.multiple_of(off_ref[(k * N + i) * N + j], T)
                rows.append(g_ref[pl.ds(at, T), :])
            r = dot(q, jnp.concatenate(rows, 0), NT)
            out[i] = r[:R] + (r[R : 2 * R] + r[2 * R :])


def tokens(off, q, g):
    return pl.pallas_call(
        tokens_kernel,
        out_shape=[shape((N, R, N * T))] * 2,
        in_specs=[SMEM, WHOLE, WHOLE],
        out_specs=[WHOLE] * 2,
        compiler_params=params(),
        cost_estimate=cost(2 * 256 * F * D, 5 << 20),
    )(off, q, g)


def errors_kernel(q_ref, e_ref, out_ref):
    q = jnp.concatenate(split(q_ref[...], 3), 0)
    e1, e2 = split(e_ref[...], 2)
    r, s = dot(q, e1, NT), dot(q[: 2 * R], e2, NT)
    out_ref[0] = r[:R] + ((r[R : 2 * R] + s[:R]) + (r[2 * R :] + s[R:]))


def errors(q, e):
    return pl.pallas_call(
        errors_kernel,
        grid=(2 * N,),
        out_shape=shape((2 * N, R, D // 8)),
        in_specs=[pl.BlockSpec((R, F), lambda i: (0, 0)), pl.BlockSpec((D // 8, F), lambda i: (i, 0))],
        out_specs=pl.BlockSpec((1, R, D // 8), lambda i: (i, 0, 0)),
        compiler_params=params(),
        cost_estimate=cost(4 * 256 * F * D, 9 << 20),
    )(q, e)


def turn_kernel(a_ref, b_ref, out_ref):
    out_ref[:, :T] = a_ref[...].T
    out_ref[:, T:] = b_ref[...].T


def turn(a, b):
    return pl.pallas_call(
        turn_kernel,
        grid=(4,),
        out_shape=shape((D, 2 * T), BF16),
        in_specs=[pl.BlockSpec((T, D // 4), lambda i: (0, i))] * 2,
        out_specs=pl.BlockSpec((D // 4, 2 * T), lambda i: (i, 0)),
        compiler_params=params(),
        cost_estimate=cost(1e9, 4 << 20),
    )(a, b)


def turn3_kernel(a_ref, b_ref, c_ref, out_ref):
    out_ref[:, :T] = a_ref[...].T
    out_ref[:, T:] = jnp.concatenate([b_ref[...], c_ref[...]], 0).T


def turn3(a, b, c):
    half = pl.BlockSpec((T // 2, D // 4), lambda i: (0, i))
    return pl.pallas_call(
        turn3_kernel,
        grid=(4,),
        out_shape=shape((D, 2 * T), BF16),
        in_specs=[pl.BlockSpec((T, D // 4), lambda i: (0, i)), half, half],
        out_specs=pl.BlockSpec((D // 4, 2 * T), lambda i: (i, 0)),
        compiler_params=params(),
        cost_estimate=cost(1e9, 4 << 20),
    )(a, b, c)


def sketch_kernel(pos_ref, h0, h1, h2, h3, e_ref, g0_ref, g1_ref, own_ref, other_ref):
    c, z = pos_ref[0], pos_ref[1]
    h = (h0[...] + h3[...]) + (h1[...] + h2[...])
    n = D // 8
    for k, out in enumerate((own_ref, other_ref)):
        for i in range(N):
            chunk = (c ^ k) * N + (z + i) % N
            rows = pl.ds(pl.multiple_of(chunk * n, n), n)
            x = jnp.concatenate([g0_ref[rows, :], g1_ref[rows, :]], 1)
            out[i] = dot_left(h, x, NT) + e_ref[chunk]


def sketch_part(pos, h, e, g0, g1):
    return pl.pallas_call(
        sketch_kernel,
        out_shape=[shape((N, R, D // 8))] * 2,
        in_specs=[SMEM] + [WHOLE] * 7,
        out_specs=[WHOLE] * 2,
        compiler_params=params(),
        cost_estimate=cost(2 * 256 * F * D, 6 << 20),
    )(pos, *h, e, g0, g1)


def add_kernel(a_ref, b_ref, *outs):
    for i, out in enumerate(outs):
        out[...] = a_ref[i] + b_ref[i]


def add_parts(a, b):
    return pl.pallas_call(
        add_kernel,
        out_shape=[shape(a.shape[1:])] * N,
        in_specs=[WHOLE] * 2,
        out_specs=[WHOLE] * N,
        compiler_params=params(),
        cost_estimate=cost(1e6, 3 * a.size * 4),
    )(a, b)


def basis_kernel(pos_ref, mine_ref, other_ref, out_ref, s_ref):
    c, z = pos_ref[0], pos_ref[1]
    n = D // 8
    for half, ref in ((1 - c, mine_ref), (c, other_ref)):
        for i, d in enumerate(OFFSETS):
            chunk = half * N + (z + d + N) % N
            s_ref[:, pl.ds(pl.multiple_of(chunk * n, n), n)] = ref[i] * 0.25
    s = s_ref[...]
    gram = dot_both(s, s, NT)
    row = lax.broadcasted_iota(jnp.int32, (R, 2 * R), 0)
    col = lax.broadcasted_iota(jnp.int32, (R, 2 * R), 1)
    work = jnp.concatenate([gram, jnp.zeros((R, R), F32)], 1) + jnp.where(col == row + R, 1.0, 0.0)
    done = jnp.zeros((R, 2 * R), F32)
    for j in range(R):
        inv = 1.0 / jnp.sqrt(work[j : j + 1, j : j + 1])
        line = work[j : j + 1, :] * inv
        done = jnp.where(row == j, line, done)
        work = work - jnp.where(row > j, work[:, j : j + 1] * inv, 0.0) * line
    out_ref[...] = dot_both(done[:, R:], s, (((1,), (0,)), ((), ())))


def basis(pos, mine, other):
    return pl.pallas_call(
        basis_kernel,
        out_shape=shape((R, D)),
        in_specs=[SMEM, WHOLE, WHOLE],
        out_specs=WHOLE,
        scratch_shapes=[pltpu.VMEM((R, D), F32)],
        compiler_params=params(),
        cost_estimate=cost(8e9, 1 << 20),
    )(pos, mine, other)


def merge_kernel(n, last, off_ref, *refs):
    acc_ref, refs = refs[0], refs[1:]
    xs, gs, refs = refs[:n], refs[n : 3 * n], refs[3 * n :]
    total = acc_ref[...]
    for i in range(n):
        total += dot(xs[i][...], jnp.concatenate([gs[2 * i][...], gs[2 * i + 1][...]], 0))
    if not last:
        refs[0][...] = total
        return
    p_ref, out_ref, q_ref = refs
    out_ref[...] = total

    @pl.when(pl.program_id(0) == 0)
    def _():
        q_ref[...] = jnp.zeros_like(q_ref)

    p = jnp.concatenate(split(p_ref[...], 3), 0)
    t1, t2 = split(total, 2)
    a, b = dot(p, t1), dot(p[: 2 * R], t2)
    q_ref[...] += a[:R] + ((a[R : 2 * R] + b[:R]) + (a[2 * R :] + b[R:]))


def merge(off, acc, groups, g, p=None, rows=512):
    n, last = len(groups), p is not None
    tile = lambda i, off: (i, 0)
    starts = tuple(s for s, _ in groups)
    at = lambda k: pl.BlockSpec((T, F), lambda i, off: (off[k] // T, 0))
    in_specs = [pl.BlockSpec((rows, F), tile)]
    in_specs += [pl.BlockSpec((rows, 2 * T), tile)] * n
    for s in starts:
        in_specs += [at(s), at(s + 1)]
    out_shape, out_specs = [shape((D, F))], [pl.BlockSpec((rows, F), tile)]
    args = [acc] + [x for _, x in groups] + [g] * (2 * n)
    if last:
        in_specs.append(pl.BlockSpec((R, rows), lambda i, off: (0, i)))
        out_shape.append(shape((R, F)))
        out_specs.append(pl.BlockSpec((R, F), lambda i, off: (0, 0)))
        args.append(p)
    return pl.pallas_call(
        functools.partial(merge_kernel, n, last),
        grid_spec=pltpu.PrefetchScalarGridSpec(
            num_scalar_prefetch=1, grid=(D // rows,), in_specs=in_specs, out_specs=out_specs
        ),
        out_shape=out_shape,
        compiler_params=params(),
        cost_estimate=cost(2 * 256 * n * D * F, (16 << 20) + n * (2 << 20)),
    )(off, *args)


def final_kernel(m_ref, p_ref, q0, q1, q2, q3, out_ref, q_ref):
    q = ((q0[...] + q3[...]) + (q1[...] + q2[...])) * 0.25
    q_ref[...] = q
    p1, p2 = split(p_ref[...], 2)
    s1, s2 = split(q, 2)
    out_ref[...] = m_ref[...] - dot(jnp.concatenate([p1, p1, p2], 0), jnp.concatenate([s1, s2, s1], 0), TN)


def final(merged, p, q, rows=512):
    whole = pl.BlockSpec((R, F), lambda i: (0, 0))
    return pl.pallas_call(
        final_kernel,
        grid=(D // rows,),
        in_specs=[pl.BlockSpec((rows, F), lambda i: (i, 0)), pl.BlockSpec((R, rows), lambda i: (0, i))] + [whole] * N,
        out_shape=[shape((D, F)), shape((R, F))],
        out_specs=[pl.BlockSpec((rows, F), lambda i: (i, 0)), whole],
        compiler_params=params(),
        cost_estimate=cost(2 * 128 * D * F, 16 << 20),
    )(merged, p, *q)


def ring_sum(value, send):
    left, right, far = send(value, 1), send(value, -1), send(value, 2)
    return (value + far) + (left + right)


def body(x, g, e, q_init):
    me = lax.axis_index("tensor")
    pos = jnp.stack([me % 2, lax.axis_index("dp")]).astype(jnp.int32)
    off = lax.dynamic_index_in_dim(jnp.asarray(block_table()), me, 0, keepdims=False)
    e, q = e[0], q_init.T

    a, b = hop(x, True, 1), hop(x, True, -1)

    own, other = tokens(off, q, g)
    got = swap(other)
    h_mine, h_far, h_right, h_opp = add_parts(own, got)
    h = [h_mine, hop(h_right, False, 1), hop(h_far, False, -1), hop(h_opp, False, 2)]
    e_part = errors(q, e)

    c, d = hop(a[: T // 2], True, 1), hop(b[T // 2 :], True, -1)
    g0 = turn(x, a)
    l0, r0 = hop(g0, False, 1), hop(g0, False, -1)
    g1 = turn3(b, c, d)
    l1, r1 = hop(g1, False, 1), hop(g1, False, -1)
    o0, o1 = hop(l0, False, 1), hop(r1, False, -1)

    s_own, s_other = sketch_part(pos, h, e_part, g0, g1)
    parts = add_parts(s_own, swap(s_other))
    s = (parts[0] + hop_z(parts[2], 2)) + (hop_z(parts[1], 1) + hop_z(parts[3], -1))
    s = ring_sum(s, functools.partial(hop, first=True) if False else (lambda v, k: hop(v, True, k)))
    s = swap(s)
    s = ring_sum(s, lambda v, k: hop(v, True, k))
    stack = jnp.stack([s, hop_z(s, 1), hop_z(s, -1), hop_z(s, 2)])
    p = basis(pos, stack, swap(stack))

    acc = e
    (acc,) = merge(off, acc, [(0, g0), (2, g1), (16, swap(g0)), (18, swap(g1))], g)
    (acc,) = merge(
        off,
        acc,
        [(4, l0), (6, l1), (8, r0), (10, r1), (20, swap(l0)), (22, swap(l1)), (24, swap(r0)), (26, swap(r1))],
        g,
    )
    acc, qp = merge(off, acc, [(12, o0), (14, o1), (28, swap(o0)), (30, swap(o1))], g, p)
    qs = [qp, hop_z(qp, 1), hop_z(qp, -1), hop_z(qp, 2)]
    err, qf = final(acc, p, qs)
    return err[None], p.T, qf.T


def solution(mesh):
    in_specs = (
        P(("dp", "tensor"), None),
        P("dp", "tensor"),
        P("dp", None, "tensor"),
        P("tensor", None),
    )
    out_specs = (P("dp", None, "tensor"), P(), P("tensor", None))
    return jax.shard_map(body, mesh=mesh, in_specs=in_specs, out_specs=out_specs, check_vma=False)
```

```python
import functools

import jax
import jax.numpy as jnp
import numpy as np
from jax import lax
from jax.experimental import pallas as pl
from jax.experimental.pallas import tpu as pltpu
from jax.sharding import PartitionSpec as P

F32, BF16 = jnp.float32, jnp.bfloat16
N, R, D, F, T = 4, 32, 4096, 512, 128
OFFSETS = (0, -1, 1, 2)
MIB = 1024 * 1024
WHOLE = pl.BlockSpec(memory_space=pltpu.VMEM)
SMEM = pl.BlockSpec(memory_space=pltpu.SMEM)
NT = (((1,), (1,)), ((), ()))
TN = (((0,), (0,)), ((), ()))


def flat(x, y, c):
    return ((x % N) * N + y % N) * 2 + c


def along(x, y, c, first, d):
    return flat(x + d, y, c) if (c == 0) == first else flat(x, y + d, c)


PLANE = [(x, y, c) for x in range(N) for y in range(N) for c in range(2)]


def hop(array, first, d):
    pairs = [(flat(*p), along(*p, first, d)) for p in PLANE]
    return lax.ppermute(array, "tensor", pairs)


def swap(array):
    return lax.ppermute(array, "tensor", [(i, i ^ 1) for i in range(2 * N * N)])


def hop_z(array, bit):
    return lax.ppermute(array, "dp", [(i, i ^ bit) for i in range(N)])


def around_z(array, d):
    return lax.ppermute(array, "dp", [(i, (i + d) % N) for i in range(N)])


def twin(array, first, bit):
    pairs = []
    for x, y, c in PLANE:
        to = (x ^ bit, y, c) if (c == 0) == first else (x, y ^ bit, c)
        pairs.append((flat(x, y, c), flat(*to)))
    return lax.ppermute(array, "tensor", pairs)


def block_tables():
    table = np.zeros((2, 2 * N * N, 2, N, N), np.int32)
    for x, y, c in PLANE:
        for k in range(2):
            colour = c ^ k
            at = y if colour == 0 else x
            for i in range(N):
                for j, first in enumerate(OFFSETS):
                    for kind, second in enumerate((OFFSETS[i], (at ^ i) - at)):
                        dx, dy = (first, second) if colour == 0 else (second, first)
                        table[kind, flat(x, y, c), k, i, j] = flat(x + dx, y + dy, colour) * T
    return np.concatenate(table.reshape(2, 2 * N * N, 2 * N * N), 1)


def split(value, parts):
    pieces = []
    for _ in range(parts):
        piece = value.astype(BF16)
        pieces.append(piece)
        value = value - piece.astype(F32)
    return pieces


def dot(a, b, dims=(((1,), (0,)), ((), ()))):
    return lax.dot_general(a, b, dims, preferred_element_type=F32)


def dot_left(value, exact, dims):
    rows = value.shape[0]
    out = dot(jnp.concatenate(split(value, 3), 0), exact, dims)
    return out[:rows] + (out[rows : 2 * rows] + out[2 * rows :])


def dot_both(value, other, dims):
    rows = value.shape[0]
    a = jnp.concatenate(split(value, 3), 0)
    b1, b2, b3 = split(other, 3)
    p1, p2, p3 = dot(a, b1, dims), dot(a[: 2 * rows], b2, dims), dot(a[:rows], b3, dims)
    low = p1[2 * rows :] + p2[rows:] + p3
    return p1[:rows] + ((p1[rows : 2 * rows] + p2[:rows]) + low)


def cost(flops, nbytes):
    return pl.CostEstimate(flops=int(flops), bytes_accessed=int(nbytes), transcendentals=0)


def shape(dims, dtype=F32):
    return jax.ShapeDtypeStruct(dims, dtype)


def run(kernel, out_shape, args, in_specs, out_specs, after=(), **kw):
    n, m = len(args), len(after)
    grid = kw.pop("grid", None)
    prefetch = kw.pop("prefetch", 0)
    options = pltpu.CompilerParams(vmem_limit_bytes=kw.pop("vmem", 16) * MIB)
    any_spec = pl.BlockSpec(memory_space=pl.ANY)
    in_specs = list(in_specs) + [any_spec] * m

    def wrapped(*refs):
        kernel(*refs[:n], *refs[n + m :])

    if prefetch:
        kw["grid_spec"] = pltpu.PrefetchScalarGridSpec(
            num_scalar_prefetch=prefetch, grid=grid, in_specs=in_specs, out_specs=out_specs
        )
    else:
        kw.update(in_specs=in_specs, out_specs=out_specs)
        if grid is not None:
            kw["grid"] = grid
    return pl.pallas_call(wrapped, out_shape=out_shape, compiler_params=options, **kw)(*args, *after)


def add3(r):
    return r[:R] + (r[R : 2 * R] + r[2 * R :])


def tokens_kernel(off_ref, q_ref, g_ref, keep_ref, send_ref, other_ref):
    q = jnp.concatenate(split(q_ref[...], 3), 0)
    outs = [keep_ref.at[0], keep_ref.at[1], send_ref.at[0], send_ref.at[1]] + [other_ref.at[i] for i in range(N)]
    for k, out in enumerate(outs):
        rows = []
        for j in range(N):
            at = pl.multiple_of(off_ref[2 * N * N + k * N + j], T)
            rows.append(g_ref[pl.ds(at, T), :])
        out[...] = add3(dot(q, jnp.concatenate(rows, 0), NT))


def tokens(off, q, g):
    return run(
        tokens_kernel,
        [shape((2, R, N * T)), shape((2, R, N * T)), shape((N, R, N * T))],
        (off, q, g),
        [SMEM, WHOLE, WHOLE],
        [WHOLE] * 3,
        cost_estimate=cost(2 * 256 * F * D, 5 << 20),
    )


def errors_kernel(q_ref, e_ref, out_ref):
    q = jnp.concatenate(split(q_ref[...], 3), 0)
    n = D // 8
    for k in range(2):
        e1, e2 = split(e_ref[k * n : (k + 1) * n, :], 2)
        r, s = dot(q, e1, NT), dot(q[: 2 * R], e2, NT)
        out_ref[k] = r[:R] + ((r[R : 2 * R] + s[:R]) + (r[2 * R :] + s[R:]))


def errors(q, e, part, after):
    return run(
        errors_kernel,
        shape((N, R, D // 8)),
        (q, e),
        [pl.BlockSpec((R, F), lambda i: (0, 0)), pl.BlockSpec((D // 4, F), lambda i: (i + 2 * part, 0))],
        pl.BlockSpec((2, R, D // 8), lambda i: (i, 0, 0)),
        after,
        grid=(2,),
        vmem=58,
        cost_estimate=cost(2 * 256 * F * D, 5 << 20),
    )


def add_kernel(n, *refs):
    for i in range(n):
        refs[2 * n + i][...] = refs[i][...] + refs[n + i][...]


def add(a, b, after=()):
    n = len(a)
    return run(
        functools.partial(add_kernel, n),
        [shape(v.shape) for v in a],
        (*a, *b),
        [WHOLE] * (2 * n),
        [WHOLE] * n,
        after,
        cost_estimate=cost(1e6, sum(3 * v.size * 4 for v in a)),
    )


def add_halves_kernel(a_ref, b_ref, got_ref, keep_ref, send_ref):
    keep_ref[...] = a_ref[...] + got_ref[:2]
    send_ref[...] = b_ref[...] + got_ref[2:]


def add_halves(a, b, got, after=()):
    return run(
        add_halves_kernel,
        [shape(a.shape)] * 2,
        (a, b, got),
        [WHOLE] * 3,
        [WHOLE] * 2,
        after,
        cost_estimate=cost(1e6, 6 * a.size * 4),
    )


def add_pair_kernel(a_ref, got_ref, keep_ref, send_ref):
    keep_ref[...] = a_ref[0] + got_ref[0]
    send_ref[...] = a_ref[1] + got_ref[1]


def add_pair(a, got, after=()):
    return run(
        add_pair_kernel,
        [shape(a.shape[1:])] * 2,
        (a, got),
        [WHOLE] * 2,
        [WHOLE] * 2,
        after,
        cost_estimate=cost(1e6, 3 * a.size * 4),
    )


def halves_kernel(a, b, top, bottom):
    h = T // 2
    top[...] = a[:h, :]
    bottom[...] = b[h:, :]


def pack0_kernel(x, a, pair):
    pair[:T, :] = x[...]
    pair[T:, :] = a[...]


def pack1_kernel(b, c, d, pair):
    h = T // 2
    pair[:T, :] = b[...]
    pair[T : T + h, :] = c[...]
    pair[T + h :, :] = d[...]


def pack(kernel, args, rows, after, steps=2):
    strip = lambda n: pl.BlockSpec((n, D // steps), lambda i: (0, i))
    return run(
        kernel,
        [shape((r, D), BF16) for r in rows],
        args,
        [strip(v.shape[0]) for v in args],
        [strip(r) for r in rows],
        after,
        grid=(steps,),
        cost_estimate=cost(1e6, 4 * sum(rows) * D),
    )


def sketch_kernel(pos_ref, h0, h1, elo_ref, ehi_ref, x_ref, a_ref, b_ref, c_ref, d_ref, keep_ref, send_ref, other_ref):
    c, z = pos_ref[0], pos_ref[1]
    h = jnp.concatenate(split(h0[...] + h1[...], 3), 0)
    n = D // 8
    outs = [keep_ref.at[0], keep_ref.at[1], send_ref.at[0], send_ref.at[1]] + [other_ref.at[i] for i in range(N)]
    for k, out in enumerate(outs):
        half, part = c ^ (k // N), z ^ (k % N)
        columns = pl.ds(pl.multiple_of((half * N + part) * n, n), n)
        x = jnp.concatenate([r[:, columns] for r in (x_ref, a_ref, b_ref, c_ref, d_ref)], 0)
        out[...] = add3(dot(h, x)) + jnp.where(half == 0, elo_ref[part], ehi_ref[part])


def sketch_part(pos, h, e, xs, after):
    return run(
        sketch_kernel,
        [shape((2, R, D // 8)), shape((2, R, D // 8)), shape((N, R, D // 8))],
        (pos, *h, *e, *xs),
        [SMEM] + [WHOLE] * 9,
        [WHOLE] * 3,
        after,
        cost_estimate=cost(2 * 256 * F * D, 6 << 20),
    )


def basis_kernel(pos_ref, mine_ref, other_ref, out_ref, s_ref):
    c, z = pos_ref[0], pos_ref[1]
    n = D // 8
    for half, ref in ((1 - c, mine_ref), (c, other_ref)):
        for i in range(N):
            chunk = half * N + (z ^ i)
            s_ref[:, pl.ds(pl.multiple_of(chunk * n, n), n)] = ref[i] * 0.25
    s = s_ref[...]
    gram = dot_both(s, s, NT)
    row = lax.broadcasted_iota(jnp.int32, (R, 2 * R), 0)
    col = lax.broadcasted_iota(jnp.int32, (R, 2 * R), 1)
    work = jnp.concatenate([gram, jnp.zeros((R, R), F32)], 1) + jnp.where(col == row + R, 1.0, 0.0)
    done = jnp.zeros((R, 2 * R), F32)
    for j in range(R):
        inv = 1.0 / jnp.sqrt(work[j : j + 1, j : j + 1])
        line = work[j : j + 1, :] * inv
        done = jnp.where(row == j, line, done)
        work = work - jnp.where(row > j, work[:, j : j + 1] * inv, 0.0) * line
    out_ref[...] = dot_both(done[:, R:], s, (((1,), (0,)), ((), ())))


def basis(pos, mine, other, after):
    return run(
        basis_kernel,
        shape((R, D)),
        (pos, mine, other),
        [SMEM, WHOLE, WHOLE],
        WHOLE,
        after,
        scratch_shapes=[pltpu.VMEM((R, D), F32)],
        cost_estimate=cost(8e9, 1 << 20),
    )


def merge_kernel(n, first, rows, from_errors, off_ref, acc_ref, *refs):
    xs, gs, out_ref = refs[:n], refs[n : 3 * n], refs[-1]
    x = jnp.concatenate([r[...] for r in xs], 0)
    g = jnp.concatenate([r[...] for r in gs], 0)
    at = pl.ds(pl.multiple_of((pl.program_id(0) + first) * rows, rows), rows)
    out_ref[at, :] = (acc_ref[...] if from_errors else acc_ref[at, :]) + dot(x, g, TN)


def merge(off, errors, acc, groups, g, lo, hi, after=(), rows=512):
    n, first = len(groups), lo // rows
    tile = pl.BlockSpec((rows, F), lambda i, off: (i + first, 0))
    at = lambda k: pl.BlockSpec((T, F), lambda i, off: (off[k] // T, 0))
    in_specs = [WHOLE if errors is None else tile]
    in_specs += [pl.BlockSpec((2 * T, rows), lambda i, off: (0, i + first))] * n
    for s, _ in groups:
        in_specs += [at(s), at(s + 1)]
    args = [off, acc if errors is None else errors] + [x for _, x in groups] + [g] * (2 * n)
    alias = {}
    if errors is None:
        alias = {1: 0}
    elif acc is not None:
        alias = {len(args): 0}
        after = (acc, *after)
    return run(
        functools.partial(merge_kernel, n, first, rows, errors is not None),
        pltpu.VMEM((D, F), F32),
        args,
        in_specs,
        WHOLE,
        after,
        prefetch=1,
        grid=((hi - lo) // rows,),
        vmem=24 if errors is None else 50,
        input_output_aliases=alias,
        cost_estimate=cost(2 * 256 * n * (hi - lo) * F, (hi - lo) * 4096 + n * (hi - lo) * 512),
    )


def right_kernel(p_ref, m_ref, q_ref):
    total, n = jnp.zeros((R, F), F32), 512
    for k in range(D // n):
        p = jnp.concatenate(split(p_ref[:, k * n : (k + 1) * n], 3), 0)
        t1, t2 = split(m_ref[k * n : (k + 1) * n, :], 2)
        a, b = dot(p, t1), dot(p[: 2 * R], t2)
        total += a[:R] + ((a[R : 2 * R] + b[:R]) + (a[2 * R :] + b[R:]))
    q_ref[...] = total


def right_part(p, merged, after):
    return run(
        right_kernel,
        shape((R, F)),
        (p, merged),
        [WHOLE] * 2,
        WHOLE,
        after,
        cost_estimate=cost(4 * 256 * D * F, 9 << 20),
    )


def right_rest_kernel(n, off_ref, p_ref, q_ref, g_ref, *refs):
    xs, out_ref = refs[:n], refs[n]
    p = jnp.concatenate(split(p_ref[...], 3), 0)
    total = q_ref[...]
    for i, (start, x) in enumerate(zip(RIGHT_STARTS, xs)):
        y = jnp.concatenate(split(add3(dot(p, x[...], NT)), 3), 0)
        rows = [g_ref[pl.ds(pl.multiple_of(off_ref[start + k], T), T), :] for k in range(2)]
        total += add3(dot(y, jnp.concatenate(rows, 0)))
    out_ref[...] = total


RIGHT_STARTS = (12, 28, 14, 30)


def right_rest(off, p, q, g, xs, after=()):
    return run(
        functools.partial(right_rest_kernel, len(xs)),
        shape((R, F)),
        (off, p, q, g, *xs),
        [SMEM] + [WHOLE] * (3 + len(xs)),
        WHOLE,
        after,
        vmem=24,
        cost_estimate=cost(2 * 256 * len(xs) * 256 * D, 14 << 20),
    )


def final_kernel(n, rows, off_ref, m_ref, *refs):
    xs, gs, (p_ref, q0, q1, q2, q3, out_ref, q_ref) = refs[:n], refs[n : 3 * n], refs[3 * n :]
    q = ((q0[...] + q1[...]) + (q2[...] + q3[...])) * 0.25
    q_ref[...] = q
    p1, p2 = split(p_ref[...], 2)
    s1, s2 = split(-q, 2)
    left = jnp.concatenate([r[...] for r in xs] + [p1, p1, p2], 0)
    right = jnp.concatenate([r[...] for r in gs] + [s1, s2, s1], 0)
    at = pl.ds(pl.multiple_of(pl.program_id(0) * rows, rows), rows)
    out_ref[...] = m_ref[at, :] + dot(left, right, TN)


def final(off, merged, groups, g, p, q, rows=512):
    n = len(groups)
    whole = pl.BlockSpec((R, F), lambda i, off: (0, 0))
    at = lambda k: pl.BlockSpec((T, F), lambda i, off: (off[k] // T, 0))
    in_specs = [WHOLE] + [pl.BlockSpec((2 * T, rows), lambda i, off: (0, i))] * n
    for s, _ in groups:
        in_specs += [at(s), at(s + 1)]
    return run(
        functools.partial(final_kernel, n, rows),
        [shape((D, F)), shape((R, F))],
        [off, merged] + [x for _, x in groups] + [g] * (2 * n) + [p, *q],
        in_specs + [pl.BlockSpec((R, rows), lambda i, off: (0, i))] + [whole] * N,
        [pl.BlockSpec((rows, F), lambda i, off: (i, 0)), whole],
        prefetch=1,
        grid=(D // rows,),
        vmem=24,
        cost_estimate=cost(2 * 256 * n * D * F, 16 << 20),
    )


def later(array, behind):
    return lax.optimization_barrier((array, behind))[0]


def body(x, g, e, q_init):
    me = lax.axis_index("tensor")
    pos = jnp.stack([me % 2, lax.axis_index("dp")]).astype(jnp.int32)
    off = lax.dynamic_index_in_dim(jnp.asarray(block_tables()), me, 0, keepdims=False)
    e, q = e[0], q_init.T

    a, b = hop(x, True, 1), hop(x, True, -1)
    keep, send, other = tokens(off, q, g)
    keep, send = add_halves(keep, send, swap(other))
    got = twin(send, False, 2)
    e_lo = errors(q, e, 0, (send,))
    h, send = add_pair(keep, got, (e_lo,))
    h_got = twin(send, False, 1)

    top, bottom = pack(halves_kernel, (a, b), (T // 2, T // 2), (send,))
    c, d = hop(top, True, 1), hop(bottom, True, -1)
    (g0,) = pack(pack0_kernel, (x, a), (2 * T,), (h_got, top))
    l0, r0 = hop(g0, False, 1), hop(g0, False, -1)
    e_hi = errors(q, e, 1, (g0,))
    keep, send, other = sketch_part(pos, (h, h_got), (e_lo, e_hi), (x, a, b, c, d), (e_hi,))
    got = swap(other)
    (g1,) = pack(pack1_kernel, (b, c, d), (2 * T,), (other,))
    l1, r1 = hop(g1, False, 1), hop(g1, False, -1)

    keep, send = add_halves(keep, send, got, (g1,))
    got = hop_z(send, 2)
    t0, t1 = swap(later(g0, send)), swap(later(g1, send))
    near = [(0, g0), (2, g1), (16, t0), (18, t1)]
    acc = merge(off, e, None, near, g, 0, 2048, (send,))
    keep, send = add_pair(keep, got, (acc,))
    got = hop_z(send, 1)
    acc = merge(off, e, acc, near, g, 2048, 4096, (send,))
    (s,) = add([keep], [got], (acc,))
    got = twin(s, True, 1)
    l0, r0 = later(l0, s), later(r0, s)
    u0, v0 = swap(l0), swap(r0)
    o0 = hop(l0, False, 1)
    (s,) = add([s], [got], ())
    got = twin(s, True, 2)
    mid = [(4, l0), (8, r0), (20, u0), (24, v0)]
    acc = merge(off, None, acc, mid, g, 0, 2048, (s,))
    (s,) = add([s], [got], (acc,))
    s = swap(s)
    got = twin(s, True, 1)
    acc = merge(off, None, acc, mid, g, 2048, 4096, (s,))
    (s,) = add([s], [got], (acc,))
    got = twin(s, True, 2)
    (s,) = add([s], [got], (acc,))
    got = hop_z(s, 1)
    l1, r1 = later(l1, s), later(r1, s)
    o1 = hop(r1, False, -1)
    u1, v1 = swap(l1), swap(r1)
    far = [(6, l1), (10, r1), (22, u1), (26, v1)]
    acc = merge(off, None, acc, far, g, 0, 2048, (s,))
    pair = later(jnp.stack([s, got]), acc)
    got = hop_z(pair, 2)
    acc = merge(off, None, acc, far, g, 2048, 4096, (pair,))
    stack = later(jnp.concatenate([pair, got]), acc)
    p = basis(pos, stack, swap(stack), (acc,))

    qp = right_part(p, acc, ())
    o0, o1 = later(o0, qp), later(o1, qp)
    last = [(12, o0), (28, swap(o0)), (14, o1), (30, swap(o1))]
    qp = right_rest(off, p, qp, g, [v for _, v in last])
    qs = (qp, around_z(qp, 2), around_z(qp, 1), around_z(qp, -1))
    err, qf = final(off, acc, last, g, p, qs)
    return err[None], p.T, qf.T


def solution(mesh):
    in_specs = (
        P(("dp", "tensor"), None),
        P("dp", "tensor"),
        P("dp", None, "tensor"),
        P("tensor", None),
    )
    out_specs = (P("dp", None, "tensor"), P(), P("tensor", None))
    return jax.shard_map(body, mesh=mesh, in_specs=in_specs, out_specs=out_specs, check_vma=False)
```

```python
import functools

import jax
import jax.numpy as jnp
import numpy as np
from jax import lax
from jax.experimental import pallas as pl
from jax.experimental.pallas import tpu as pltpu
from jax.sharding import PartitionSpec as P

F32, BF16 = jnp.float32, jnp.bfloat16
N, R, D, F, T = 4, 32, 4096, 512, 128
OFFSETS = (0, -1, 1, 2)
MIB = 1024 * 1024
WHOLE = pl.BlockSpec(memory_space=pltpu.VMEM)
SMEM = pl.BlockSpec(memory_space=pltpu.SMEM)
HBM = pl.BlockSpec(memory_space=pltpu.HBM)
NT = (((1,), (1,)), ((), ()))
TN = (((0,), (0,)), ((), ()))


def flat(x, y, c):
    return ((x % N) * N + y % N) * 2 + c


def along(x, y, c, first, d):
    return flat(x + d, y, c) if (c == 0) == first else flat(x, y + d, c)


PLANE = [(x, y, c) for x in range(N) for y in range(N) for c in range(2)]


def hop(array, first, d):
    pairs = [(flat(*p), along(*p, first, d)) for p in PLANE]
    return lax.ppermute(array, "tensor", pairs)


def swap(array):
    return lax.ppermute(array, "tensor", [(i, i ^ 1) for i in range(2 * N * N)])


def hop_z(array, bit):
    return lax.ppermute(array, "dp", [(i, i ^ bit) for i in range(N)])


def around_z(array, d):
    return lax.ppermute(array, "dp", [(i, (i + d) % N) for i in range(N)])


def twin(array, first, bit):
    pairs = []
    for x, y, c in PLANE:
        to = (x ^ bit, y, c) if (c == 0) == first else (x, y ^ bit, c)
        pairs.append((flat(x, y, c), flat(*to)))
    return lax.ppermute(array, "tensor", pairs)


def block_tables():
    offsets = np.zeros((2 * N * N, 2, N, N, 2), np.int32)
    moved = np.zeros((2 * N * N, N * N * 2), np.int32)
    for x, y, c in PLANE:
        at = y if c == 0 else x
        for i in range(N):
            for j, first in enumerate(OFFSETS):
                for kind, second in enumerate((OFFSETS[i], (at ^ i) - at)):
                    dx, dy = (first, second) if c == 0 else (second, first)
                    for m in range(2):
                        offsets[flat(x, y, c), kind, i, j, m] = flat(x + dx, y + dy, c ^ m) * T
    for x, y, c in PLANE:
        here = offsets[flat(x, y, c), 1].reshape(-1).tolist()
        there = offsets[flat(x, y, 1 - c), 1].reshape(-1).tolist()
        moved[flat(x, y, c)] = [here.index(row) for row in there]
    return np.concatenate([offsets.reshape(2 * N * N, -1), moved], 1)


def split(value, parts):
    pieces = []
    for _ in range(parts):
        piece = value.astype(BF16)
        pieces.append(piece)
        value = value - piece.astype(F32)
    return pieces


def dot(a, b, dims=(((1,), (0,)), ((), ()))):
    return lax.dot_general(a, b, dims, preferred_element_type=F32)


def dot_left(value, exact, dims):
    rows = value.shape[0]
    out = dot(jnp.concatenate(split(value, 3), 0), exact, dims)
    return out[:rows] + (out[rows : 2 * rows] + out[2 * rows :])


def dot_both(value, other, dims):
    rows = value.shape[0]
    a = jnp.concatenate(split(value, 3), 0)
    b1, b2, b3 = split(other, 3)
    p1, p2, p3 = dot(a, b1, dims), dot(a[: 2 * rows], b2, dims), dot(a[:rows], b3, dims)
    low = p1[2 * rows :] + p2[rows:] + p3
    return p1[:rows] + ((p1[rows : 2 * rows] + p2[:rows]) + low)


def shape(dims, dtype=F32):
    return jax.ShapeDtypeStruct(dims, dtype)


def run(kernel, out_shape, args, in_specs, out_specs, after=(), **kw):
    n, m = len(args), len(after)
    grid = kw.pop("grid", None)
    kw["cost_estimate"] = pl.CostEstimate(flops=1000, bytes_accessed=1000, transcendentals=0)
    prefetch = kw.pop("prefetch", 0)
    options = pltpu.CompilerParams(vmem_limit_bytes=kw.pop("vmem", 16) * MIB)
    any_spec = pl.BlockSpec(memory_space=pl.ANY)
    in_specs = list(in_specs) + [any_spec] * m

    def wrapped(*refs):
        kernel(*refs[:n], *refs[n + m :])

    if prefetch:
        kw["grid_spec"] = pltpu.PrefetchScalarGridSpec(
            num_scalar_prefetch=prefetch,
            grid=grid,
            in_specs=in_specs,
            out_specs=out_specs,
            scratch_shapes=kw.pop("scratch_shapes", ()),
        )
    else:
        kw.update(in_specs=in_specs, out_specs=out_specs)
        if grid is not None:
            kw["grid"] = grid
    return pl.pallas_call(wrapped, out_shape=out_shape, compiler_params=options, **kw)(*args, *after)


def add3(r):
    return r[:R] + (r[R : 2 * R] + r[2 * R :])


H = D // 2
B = 2 * N * N


def tokens_kernel(off_ref, q_ref, g_ref, keep_ref, send_ref, other_ref, h_ref):
    q = jnp.concatenate(split(q_ref[...], 3), 0)
    for k in range(N * 2):
        rows = [g_ref[pl.ds(pl.multiple_of(off_ref[B + k * N + j], T), T), :] for j in range(N)]
        r = add3(dot(q, jnp.concatenate(rows, 0), NT))
        for j in range(N):
            h_ref[k * N + j] = r[:, j * T : (j + 1) * T]
    for i in range(N):
        out = (keep_ref if i < 2 else send_ref).at[i % 2]
        for k in range(2 * N):
            out[:, k * T : (k + 1) * T] = h_ref[i * 2 * N + k]
            other_ref[i, :, k * T : (k + 1) * T] = h_ref[off_ref[2 * B + i * 2 * N + k]]


def tokens(off, q, g, after):
    w = 2 * N * T
    return run(
        tokens_kernel,
        [shape((2, R, w)), shape((2, R, w)), shape((N, R, w))],
        (off, q, g),
        [SMEM, WHOLE, WHOLE],
        [WHOLE] * 3,
        after,
        scratch_shapes=[pltpu.VMEM((B, R, T), F32)],
    )


def fetches(e_ref, half, buf_ref, sems, parts=range(N)):
    n = H // N
    return [
        pltpu.make_async_copy(
            e_ref.at[pl.ds(pl.multiple_of(half * H + k * n, n), n), :], buf_ref.at[pl.ds(k * n, n), :], sems.at[k]
        )
        for k in parts
    ]


FETCH = [pltpu.VMEM((H, F), F32), pltpu.SemaphoreType.DMA((N,))]


def errors_kernel(other, pos_ref, q_ref, e_ref, out_ref, buf_ref, sems):
    copies = fetches(e_ref, pos_ref[0] ^ other, buf_ref, sems)
    for copy in copies:
        copy.start()
    q = jnp.concatenate(split(q_ref[...], 3), 0)
    n = H // N
    for k in range(N):
        copies[k].wait()
        e1, e2 = split(buf_ref[k * n : (k + 1) * n, :], 2)
        r, s = dot(q, e1, NT), dot(q[: 2 * R], e2, NT)
        out_ref[k] = r[:R] + ((r[R : 2 * R] + s[:R]) + (r[2 * R :] + s[R:]))


def errors(pos, q, e, other, after):
    return run(
        functools.partial(errors_kernel, other),
        shape((N, R, D // 8)),
        (pos, q, e),
        [SMEM, WHOLE, HBM],
        WHOLE,
        after,
        scratch_shapes=FETCH,
    )


def add_kernel(n, *refs):
    for i in range(n):
        refs[2 * n + i][...] = refs[i][...] + refs[n + i][...]


def add(a, b, after=()):
    n = len(a)
    return run(
        functools.partial(add_kernel, n),
        [shape(v.shape) for v in a],
        (*a, *b),
        [WHOLE] * (2 * n),
        [WHOLE] * n,
        after,
    )


def add_halves_kernel(a_ref, b_ref, got_ref, keep_ref, send_ref):
    keep_ref[...] = a_ref[...] + got_ref[:2]
    send_ref[...] = b_ref[...] + got_ref[2:]


def add_halves(a, b, got, after=()):
    return run(
        add_halves_kernel,
        [shape(a.shape)] * 2,
        (a, b, got),
        [WHOLE] * 3,
        [WHOLE] * 2,
        after,
    )


def add_pair_kernel(a_ref, got_ref, keep_ref, send_ref):
    keep_ref[...] = a_ref[0] + got_ref[0]
    send_ref[...] = a_ref[1] + got_ref[1]


def add_pair(a, got, after=()):
    return run(
        add_pair_kernel,
        [shape(a.shape[1:])] * 2,
        (a, got),
        [WHOLE] * 2,
        [WHOLE] * 2,
        after,
    )


def cut_kernel(pos_ref, x_ref, mine_ref, send_ref):
    at = pl.multiple_of(pos_ref[0] * H, H)
    mine_ref[...] = x_ref[:, pl.ds(at, H)]
    send_ref[...] = x_ref[:, pl.ds(H - at, H)]


def cut(pos, x):
    return run(cut_kernel, [shape((T, H), BF16)] * 2, (pos, x), [SMEM, WHOLE], [WHOLE] * 2)


def halves_kernel(a, b, top, bottom):
    top[...] = a[:T, :]
    bottom[...] = b[T:, :]


def stack_kernel(*refs):
    *parts, out = refs
    at = 0
    for part in parts:
        out[at : at + part.shape[0], :] = part[...]
        at += part.shape[0]


def pack(kernel, args, rows, after):
    return run(kernel, [shape((r, H), BF16) for r in rows], args, [WHOLE] * len(args), [WHOLE] * len(rows), after)


def held_kernel(in_ref, out_ref):
    out_ref[...] = in_ref[...]


def held(array, after):
    return run(held_kernel, pltpu.VMEM(array.shape, array.dtype), (array,), [WHOLE], WHOLE, after)


def sketch_kernel(pos_ref, h0, h1, e0_ref, e1_ref, x0_ref, x1_ref, keep_ref, send_ref):
    z = pos_ref[1]
    h = jnp.concatenate(split(h0[...] + h1[...], 3), 0)
    n = D // 8
    for i in range(N):
        part = z ^ i
        columns = pl.ds(pl.multiple_of(part * n, n), n)
        x = jnp.concatenate([x0_ref[:, columns], x1_ref[:, columns]], 0)
        (keep_ref if i < 2 else send_ref)[i % 2] = add3(dot(h, x)) + (e0_ref[part] + e1_ref[part])


def sketch_part(pos, h, e, xs, after):
    return run(
        sketch_kernel,
        [shape((2, R, D // 8))] * 2,
        (pos, *h, *e, *xs),
        [SMEM] + [WHOLE] * 6,
        [WHOLE] * 2,
        after,
    )


def basis_kernel(pos_ref, mine_ref, other_ref, out_ref, s_ref):
    c, z = pos_ref[0], pos_ref[1]
    n = D // 8
    for half, ref in ((1 - c, mine_ref), (c, other_ref)):
        for i in range(N):
            chunk = half * N + (z ^ i)
            s_ref[:, pl.ds(pl.multiple_of(chunk * n, n), n)] = ref[i] * 0.25
    s = s_ref[...]
    gram = dot_both(s, s, NT)
    row = lax.broadcasted_iota(jnp.int32, (R, 2 * R), 0)
    col = lax.broadcasted_iota(jnp.int32, (R, 2 * R), 1)
    work = jnp.concatenate([gram, jnp.zeros((R, R), F32)], 1) + jnp.where(col == row + R, 1.0, 0.0)
    for j in range(R - 1):
        column = jnp.broadcast_to(work[:, j : j + 1], (R, 2 * R))
        line = work[j : j + 1, :] / column[j : j + 1, :]
        work = work - jnp.where(row > j, column, 0.0) * line
    pivot = jnp.sum(jnp.where(row == col, work, 0.0), 1, keepdims=True)
    done = work / jnp.sqrt(pivot)
    out_ref[...] = dot_both(done[:, R:], s, (((1,), (0,)), ((), ())))


def basis(pos, mine, other, after):
    return run(
        basis_kernel,
        pltpu.VMEM((R, D), F32),
        (pos, mine, other),
        [SMEM, WHOLE, WHOLE],
        WHOLE,
        after,
        scratch_shapes=[pltpu.VMEM((R, D), F32)],
    )


def block_rows(off_ref, g_ref, starts):
    rows = [pl.ds(pl.multiple_of(off_ref[start + k], T), T) for start in starts for k in range(4)]
    return jnp.concatenate([g_ref[at, :] for at in rows], 0)


def merge_kernel(starts, lo, hi, has_errors, has_acc, off_ref, pos_ref, g_ref, go_ref, *refs):
    n, step = len(starts), H // N
    xs, refs = refs[:n], list(refs[n:])
    e_ref = refs.pop(0) if has_errors else None
    own_in, other_in = (refs.pop(0), refs.pop(0)) if has_acc else (None, None)
    own_ref, other_ref = refs[:2]
    if has_errors:
        copies = fetches(e_ref, pos_ref[0], refs[2], refs[3], range(lo // step, hi // step))
        for copy in copies:
            copy.start()
    rows = jnp.concatenate([block_rows(off_ref, g_ref, starts), block_rows(off_ref, go_ref, starts)], 1)
    for k in range((hi - lo) // step):
        at = slice(lo + k * step, lo + (k + 1) * step)
        product = dot(jnp.concatenate([r[:, at] for r in xs], 0), rows, TN)
        if has_errors:
            copies[k].wait()
            own_ref[at, :] = refs[2][at, :] + product[:, :F]
            other_ref[at, :] = product[:, F:]
        else:
            own_ref[at, :] = own_in[at, :] + product[:, :F]
            other_ref[at, :] = other_in[at, :] + product[:, F:]


def merge(off, pos, g, g_other, groups, lo, hi, errors=None, acc=None, after=()):
    starts, xs = [start for start, _ in groups], [x for _, x in groups]
    args = [off, pos, g, g_other, *xs] + ([] if errors is None else [errors]) + ([] if acc is None else [*acc])
    specs = [SMEM] * 2 + [WHOLE] * (2 + len(xs)) + ([] if errors is None else [HBM]) + [WHOLE] * (2 if acc else 0)
    return run(
        functools.partial(merge_kernel, starts, lo, hi, errors is not None, acc is not None),
        [pltpu.VMEM((H, F), F32)] * 2,
        args,
        specs,
        [WHOLE] * 2,
        after,
        scratch_shapes=() if errors is None else FETCH,
        input_output_aliases={} if acc is None else {len(args) - 2: 0, len(args) - 1: 1},
    )


def last_other_kernel(starts, off_ref, acc_ref, g_ref, *refs):
    *xs, out_ref = refs
    rows, step = block_rows(off_ref, g_ref, starts), H // N
    for k in range(N):
        at = slice(k * step, (k + 1) * step)
        out_ref[at, :] = acc_ref[at, :] + dot(jnp.concatenate([r[:, at] for r in xs], 0), rows, TN)


def last_other(off, acc, groups, g, after):
    return run(
        functools.partial(last_other_kernel, [start for start, _ in groups]),
        pltpu.VMEM((H, F), F32),
        (off, acc, g, *[x for _, x in groups]),
        [SMEM] + [WHOLE] * (2 + len(groups)),
        WHOLE,
        after,
    )


def p_times(p, m):
    t1, t2 = split(m, 2)
    a, b = dot(p, t1), dot(p[: 2 * R], t2)
    return a[:R] + ((a[R : 2 * R] + b[:R]) + (a[2 * R :] + b[R:]))


def right_kernel(pos_ref, p_ref, own_ref, other_ref, e_ref, q_ref, send_ref, buf_ref, sems):
    copies = fetches(e_ref, 1 - pos_ref[0], buf_ref, sems)
    for copy in copies:
        copy.start()
    n = H // N
    q, send = jnp.zeros((R, F), F32), jnp.zeros((R, F), F32)
    for k in range(N):
        at = pl.ds(pl.multiple_of(pos_ref[0] * H + k * n, n), n)
        p = jnp.concatenate(split(p_ref[:, at], 3), 0)
        q += p_times(p, own_ref[k * n : (k + 1) * n, :])
        send += p_times(p, other_ref[k * n : (k + 1) * n, :])
    for k in range(N):
        at = pl.ds(pl.multiple_of((1 - pos_ref[0]) * H + k * n, n), n)
        p = jnp.concatenate(split(p_ref[:, at], 3), 0)
        copies[k].wait()
        q += p_times(p, buf_ref[k * n : (k + 1) * n, :])
    q_ref[...] = q
    send_ref[...] = send


def right_part(pos, p, acc, e, after):
    return run(
        right_kernel,
        [shape((R, F))] * 2,
        (pos, p, *acc, e),
        [SMEM] + [WHOLE] * 3 + [HBM],
        [WHOLE] * 2,
        after,
        scratch_shapes=FETCH,
    )


def right_rest_kernel(starts, off_ref, pos_ref, p_ref, q_ref, send_ref, g_ref, go_ref, *refs):
    n = len(starts)
    xs, (out_ref, out_send_ref) = refs[:n], refs[n:]
    here = pl.ds(pl.multiple_of(pos_ref[0] * H, H), H)
    p = jnp.concatenate(split(p_ref[:, here], 3), 0)
    total, send = q_ref[...], send_ref[...]
    for start, x in zip(starts, xs):
        y = dot(x[...], p, NT)
        y = jnp.concatenate(split(y[:, :R] + (y[:, R : 2 * R] + y[:, 2 * R :]), 3), 1)
        rows = [pl.ds(pl.multiple_of(off_ref[start + k], T), T) for k in range(4)]
        total += add3(dot(y, jnp.concatenate([g_ref[at, :] for at in rows], 0), TN))
        send += add3(dot(y, jnp.concatenate([go_ref[at, :] for at in rows], 0), TN))
    out_ref[...] = total
    out_send_ref[...] = send


def right_rest(off, pos, p, q, send, g, g_other, groups):
    return run(
        functools.partial(right_rest_kernel, [start for start, _ in groups]),
        [shape((R, F))] * 2,
        (off, pos, p, q, send, g, g_other, *[x for _, x in groups]),
        [SMEM] * 2 + [WHOLE] * (5 + len(groups)),
        [WHOLE] * 2,
        vmem=24,
    )


def final_kernel(n, rows, starts, pos_ref, off_ref, m_ref, e_ref, got_ref, g_ref, *refs):
    xs, (p_ref, q0, q1, q2, q3, out_ref, q_ref, right_ref, buf_ref, sems) = refs[:n], refs[n:]
    copies = fetches(e_ref, 1 - pos_ref[0], buf_ref, sems)
    i, steps = pl.program_id(0), H // rows
    k = n * 4 * T

    @pl.when(i == 0)
    def _():
        for copy in copies:
            copy.start()
        q = ((q0[...] + q1[...]) + (q2[...] + q3[...])) * 0.25
        q_ref[...] = q
        s1, s2 = split(-q, 2)
        for j, start in enumerate(starts):
            for b in range(4):
                at = pl.ds(pl.multiple_of(off_ref[start + b], T), T)
                right_ref[(4 * j + b) * T : (4 * j + b + 1) * T, :] = g_ref[at, :]
        right_ref[k:, :] = jnp.concatenate([s1, s2, s1], 0)

    half = jnp.where(i < steps, pos_ref[0], 1 - pos_ref[0])
    step = lax.rem(i, steps)
    p1, p2 = split(p_ref[:, pl.ds(pl.multiple_of(half * H + step * rows, rows), rows)], 2)
    p = jnp.concatenate([p1, p1, p2], 0)
    at = pl.ds(pl.multiple_of(step * rows, rows), rows)

    @pl.when(i < steps)
    def _():
        left = jnp.concatenate([r[:, at] for r in xs] + [p], 0)
        out_ref[...] = m_ref[at, :] + dot(left, right_ref[...], TN)

    for j, copy in enumerate(copies):
        pl.when(i == steps + j * steps // N)(copy.wait)

    @pl.when(i >= steps)
    def _():
        out_ref[...] = (buf_ref[at, :] + got_ref[at, :]) + dot(p, right_ref[k:, :], TN)


def final(off, pos, own, e, got, groups, g, p, q, rows=H // 2):
    n, steps = len(groups), H // rows
    half = lambda i, pos: jnp.where(i < steps, pos[0], 1 - pos[0])
    return run(
        functools.partial(final_kernel, n, rows, [start for start, _ in groups]),
        [shape((D, F)), shape((R, F))],
        [pos, off, own, e, got, g] + [x for _, x in groups] + [p, *q],
        [
            SMEM,
            WHOLE,
            HBM,
        ]
        + [WHOLE] * (n + 3 + N),
        [
            pl.BlockSpec((rows, F), lambda i, pos: (half(i, pos) * steps + lax.rem(i, steps), 0)),
            pl.BlockSpec((R, F), lambda i, pos: (0, 0)),
        ],
        prefetch=1,
        grid=(2 * steps,),
        vmem=24,
        scratch_shapes=[pltpu.VMEM((n * 4 * T + 3 * R, F), BF16)] + FETCH,
    )


def later(array, behind):
    return lax.optimization_barrier((array, behind))[0]


def body(x, g, e, q_init):
    me = lax.axis_index("tensor")
    pos = jnp.stack([me % 2, lax.axis_index("dp")]).astype(jnp.int32)
    off = lax.dynamic_index_in_dim(jnp.asarray(block_tables()), me, 0, keepdims=False)
    e, q = pltpu.with_memory_space_constraint(e[0], pltpu.HBM), q_init.T

    mine, send = cut(pos, x)
    (x0,) = pack(stack_kernel, (mine, swap(send)), (2 * T,), ())
    a, b = hop(x0, True, 1), hop(x0, True, -1)
    g_other = swap(later(g, x0))
    keep, send, other = tokens(off, q, g, (x0,))
    got = swap(other)
    keep, send = add_halves(keep, send, got, ())
    got = twin(send, False, 2)
    e_other = errors(pos, q, e, 1, (send,))
    g_other = held(g_other, (e_other,))
    h, send = add_pair(keep, got, (g_other,))
    h_got = twin(send, False, 1)
    top, bottom = pack(halves_kernel, (a, b), (T, T), (send,))
    c, d = hop(top, True, 1), hop(bottom, True, -1)
    e_got = swap(later(e_other, top))
    e_own = errors(pos, q, e, 0, (top,))

    (g0,) = pack(stack_kernel, (x0, a), (4 * T,), (h_got, e_own))
    l0, r0 = hop(g0, False, 1), hop(g0, False, -1)
    (g1,) = pack(stack_kernel, (b, c, d), (4 * T,), (g0,))
    l1, r1 = hop(g1, False, 1), hop(g1, False, -1)

    keep, send = sketch_part(pos, (h, h_got), (e_own, e_got), (g0, g1), ())
    got = hop_z(send, 2)
    near = [(0, g0), (4, g1)]
    acc = merge(off, pos, g, g_other, near, 0, H // 2, e, None, (send,))
    keep, send = add_pair(keep, got, (acc[0],))
    got = hop_z(send, 1)
    acc = merge(off, pos, g, g_other, near, H // 2, H, e, acc, (send,))
    (s,) = add([keep], [got], (acc[0],))
    got = twin(s, True, 1)
    (s,) = add([s], [got], ())
    got = twin(s, True, 2)
    l0, r0 = later(l0, s), later(r0, s)
    o0 = hop(l0, False, 1)
    mid = [(8, l0), (16, r0)]
    acc = merge(off, pos, g, g_other, mid, 0, H // 2, None, acc, (s,))
    (s,) = add([s], [got], (acc[0],))
    s = swap(s)
    got = twin(s, True, 1)
    acc = merge(off, pos, g, g_other, mid, H // 2, H, None, acc, (s,))
    (s,) = add([s], [got], (acc[0],))
    got = twin(s, True, 2)
    (s,) = add([s], [got], ())
    got = hop_z(s, 1)
    l1, r1 = later(l1, s), later(r1, s)
    o1 = hop(r1, False, -1)
    far = [(12, l1), (20, r1)]
    acc = merge(off, pos, g, g_other, far, 0, H // 2, None, acc, (s,))
    pair = jnp.stack([later(s, acc[0]), got])
    got = hop_z(pair, 2)
    acc = merge(off, pos, g, g_other, far, H // 2, H, None, acc, (pair,))
    stack = jnp.concatenate([later(pair, acc[0]), got])
    p = basis(pos, stack, swap(stack), (acc[0],))

    last = [(24, later(o0, p)), (28, later(o1, p))]
    qp, q_send = right_part(pos, p, acc, e, ())
    qp, q_send = right_rest(off, pos, p, qp, q_send, g, g_other, last)
    q_got = swap(q_send)
    out = last_other(off, acc[1], last, g_other, (q_send,))
    (qp,) = add([qp], [q_got], (out,))
    out = swap(later(out, qp))
    qs = (qp, around_z(qp, 2), around_z(qp, 1), around_z(qp, -1))
    err, qf = final(off, pos, acc[0], e, out, last, g, p, qs)
    return err[None], p.T, qf.T


def solution(mesh):
    in_specs = (
        P(("dp", "tensor"), None),
        P("dp", "tensor"),
        P("dp", None, "tensor"),
        P("tensor", None),
    )
    out_specs = (P("dp", None, "tensor"), P(), P("tensor", None))
    return jax.shard_map(body, mesh=mesh, in_specs=in_specs, out_specs=out_specs, check_vma=False)
```

```python
import functools

import jax
import jax.numpy as jnp
import numpy as np
from jax import lax
from jax.experimental import pallas as pl
from jax.experimental.pallas import tpu as pltpu
from jax.sharding import PartitionSpec as P

F32, BF16 = jnp.float32, jnp.bfloat16
N, R, D, F, T = 4, 32, 4096, 512, 128
OFFSETS = (0, -1, 1, 2)
BITS = (0, 2, 1, 3)
MIB = 1024 * 1024
WHOLE = pl.BlockSpec(memory_space=pltpu.VMEM)
SMEM = pl.BlockSpec(memory_space=pltpu.SMEM)
HBM = pl.BlockSpec(memory_space=pltpu.HBM)
NT = (((1,), (1,)), ((), ()))
TN = (((0,), (0,)), ((), ()))


def flat(x, y, c):
    return ((x % N) * N + y % N) * 2 + c


def along(x, y, c, first, d):
    return flat(x + d, y, c) if (c == 0) == first else flat(x, y + d, c)


PLANE = [(x, y, c) for x in range(N) for y in range(N) for c in range(2)]


def hop(array, first, d):
    pairs = [(flat(*p), along(*p, first, d)) for p in PLANE]
    return lax.ppermute(array, "tensor", pairs)


def swap(array):
    return lax.ppermute(array, "tensor", [(i, i ^ 1) for i in range(2 * N * N)])


def hop_z(array, bit):
    return lax.ppermute(array, "dp", [(i, i ^ bit) for i in range(N)])


def around_z(array, d):
    return lax.ppermute(array, "dp", [(i, (i + d) % N) for i in range(N)])


def twin(array, first, bit):
    pairs = []
    for x, y, c in PLANE:
        to = (x ^ bit, y, c) if (c == 0) == first else (x, y ^ bit, c)
        pairs.append((flat(x, y, c), flat(*to)))
    return lax.ppermute(array, "tensor", pairs)


def block_tables():
    offsets = np.zeros((2 * N * N, 2, N, N, 2), np.int32)
    moved = np.zeros((2 * N * N, N * N * 2), np.int32)
    for x, y, c in PLANE:
        at = y if c == 0 else x
        for i in range(N):
            for j, first in enumerate(OFFSETS):
                for kind, second in enumerate((OFFSETS[i], (at ^ BITS[i]) - at)):
                    dx, dy = (first, second) if c == 0 else (second, first)
                    for m in range(2):
                        offsets[flat(x, y, c), kind, i, j, m] = flat(x + dx, y + dy, c ^ m) * T
    for x, y, c in PLANE:
        here = offsets[flat(x, y, c), 1].reshape(-1).tolist()
        there = offsets[flat(x, y, 1 - c), 1].reshape(-1).tolist()
        moved[flat(x, y, c)] = [here.index(row) for row in there]
    return np.concatenate([offsets.reshape(2 * N * N, -1), moved], 1)


def split(value, parts):
    pieces = []
    for _ in range(parts):
        piece = value.astype(BF16)
        pieces.append(piece)
        value = value - piece.astype(F32)
    return pieces


def dot(a, b, dims=(((1,), (0,)), ((), ()))):
    return lax.dot_general(a, b, dims, preferred_element_type=F32)


def dot_left(value, exact, dims):
    rows = value.shape[0]
    out = dot(jnp.concatenate(split(value, 3), 0), exact, dims)
    return out[:rows] + (out[rows : 2 * rows] + out[2 * rows :])


def dot_both(value, other, dims):
    rows = value.shape[0]
    a = jnp.concatenate(split(value, 3), 0)
    b1, b2, b3 = split(other, 3)
    p1, p2, p3 = dot(a, b1, dims), dot(a[: 2 * rows], b2, dims), dot(a[:rows], b3, dims)
    low = p1[2 * rows :] + p2[rows:] + p3
    return p1[:rows] + ((p1[rows : 2 * rows] + p2[:rows]) + low)


def shape(dims, dtype=F32):
    return jax.ShapeDtypeStruct(dims, dtype)


def run(kernel, out_shape, args, in_specs, out_specs, after=(), **kw):
    n, m = len(args), len(after)
    grid = kw.pop("grid", None)
    kw["cost_estimate"] = pl.CostEstimate(flops=1000, bytes_accessed=1000, transcendentals=0)
    prefetch = kw.pop("prefetch", 0)
    options = pltpu.CompilerParams(vmem_limit_bytes=kw.pop("vmem", 16) * MIB)
    any_spec = pl.BlockSpec(memory_space=pl.ANY)
    in_specs = list(in_specs) + [any_spec] * m

    def wrapped(*refs):
        kernel(*refs[:n], *refs[n + m :])

    if prefetch:
        kw["grid_spec"] = pltpu.PrefetchScalarGridSpec(
            num_scalar_prefetch=prefetch,
            grid=grid,
            in_specs=in_specs,
            out_specs=out_specs,
            scratch_shapes=kw.pop("scratch_shapes", ()),
        )
    else:
        kw.update(in_specs=in_specs, out_specs=out_specs)
        if grid is not None:
            kw["grid"] = grid
    return pl.pallas_call(wrapped, out_shape=out_shape, compiler_params=options, **kw)(*args, *after)


def add3(r):
    return r[:R] + (r[R : 2 * R] + r[2 * R :])


H = D // 2
B = 2 * N * N


def tokens_kernel(off_ref, q_ref, g_ref, own_ref, other_ref, h_ref):
    q = jnp.concatenate(split(q_ref[...], 3), 0)
    for k in range(N * 2):
        rows = [g_ref[pl.ds(pl.multiple_of(off_ref[B + k * N + j], T), T), :] for j in range(N)]
        r = add3(dot(q, jnp.concatenate(rows, 0), NT))
        for j in range(N):
            h_ref[k * N + j] = r[:, j * T : (j + 1) * T]
    for i in range(N):
        for k in range(2 * N):
            own_ref[i, :, k * T : (k + 1) * T] = h_ref[i * 2 * N + k]
            other_ref[i, :, k * T : (k + 1) * T] = h_ref[off_ref[2 * B + i * 2 * N + k]]


def tokens(off, q, g, after):
    w = 2 * N * T
    return run(
        tokens_kernel,
        [shape((N, R, w))] * 2,
        (off, q, g),
        [SMEM, WHOLE, WHOLE],
        [WHOLE] * 2,
        after,
        scratch_shapes=[pltpu.VMEM((B, R, T), F32)],
    )


def fetches(e_ref, half, buf_ref, sems, parts=range(N)):
    n = H // N
    return [
        pltpu.make_async_copy(
            e_ref.at[pl.ds(pl.multiple_of(half * H + k * n, n), n), :], buf_ref.at[pl.ds(k * n, n), :], sems.at[k]
        )
        for k in parts
    ]


FETCH = [pltpu.VMEM((H, F), F32), pltpu.SemaphoreType.DMA((N,))]


def errors_kernel(other, pos_ref, q_ref, e_ref, out_ref, buf_ref, sems):
    copies = fetches(e_ref, pos_ref[0] ^ other, buf_ref, sems)
    for copy in copies:
        copy.start()
    q = jnp.concatenate(split(q_ref[...], 3), 0)
    n = H // N
    for k in range(N):
        copies[k].wait()
        e1, e2 = split(buf_ref[k * n : (k + 1) * n, :], 2)
        r, s = dot(q, e1, NT), dot(q[: 2 * R], e2, NT)
        out_ref[k] = r[:R] + ((r[R : 2 * R] + s[:R]) + (r[2 * R :] + s[R:]))


def errors(pos, q, e, other, after):
    return run(
        functools.partial(errors_kernel, other),
        shape((N, R, D // 8)),
        (pos, q, e),
        [SMEM, WHOLE, HBM],
        WHOLE,
        after,
        scratch_shapes=FETCH,
    )


def add_kernel(n, *refs):
    for i in range(n):
        refs[2 * n + i][...] = refs[i][...] + refs[n + i][...]


def add(a, b, after=()):
    n = len(a)
    return run(
        functools.partial(add_kernel, n),
        [shape(v.shape) for v in a],
        (*a, *b),
        [WHOLE] * (2 * n),
        [WHOLE] * n,
        after,
    )


def add_parts_kernel(a_ref, b_ref, *outs):
    for i, out in enumerate(outs):
        out[...] = a_ref[i] + b_ref[i]


def add_parts(a, b, after=()):
    return run(add_parts_kernel, [shape(a.shape[1:])] * a.shape[0], (a, b), [WHOLE] * 2, [WHOLE] * a.shape[0], after)


def add_pair_kernel(a_ref, got_ref, keep_ref, send_ref):
    keep_ref[...] = a_ref[0] + got_ref[0]
    send_ref[...] = a_ref[1] + got_ref[1]


def add_pair(a, got, after=()):
    return run(
        add_pair_kernel,
        [shape(a.shape[1:])] * 2,
        (a, got),
        [WHOLE] * 2,
        [WHOLE] * 2,
        after,
    )


def cut_kernel(pos_ref, x_ref, mine_ref, send_ref):
    at = pl.multiple_of(pos_ref[0] * H, H)
    mine_ref[...] = x_ref[:, pl.ds(at, H)]
    send_ref[...] = x_ref[:, pl.ds(H - at, H)]


def cut(pos, x):
    return run(cut_kernel, [shape((T, H), BF16)] * 2, (pos, x), [SMEM, WHOLE], [WHOLE] * 2)


def halves_kernel(a, b, top, bottom):
    top[...] = a[:T, :]
    bottom[...] = b[T:, :]


def stack_kernel(*refs):
    *parts, out = refs
    at = 0
    for part in parts:
        out[at : at + part.shape[0], :] = part[...]
        at += part.shape[0]


def pack(kernel, args, rows, after):
    return run(kernel, [shape((r, H), BF16) for r in rows], args, [WHOLE] * len(args), [WHOLE] * len(rows), after)


def held_kernel(in_ref, out_ref):
    out_ref[...] = in_ref[...]


def held(array, after):
    return run(held_kernel, pltpu.VMEM(array.shape, array.dtype), (array,), [WHOLE], WHOLE, after)


def sketch_kernel(pos_ref, h0, h1, h2, h3, e0_ref, e1_ref, x0_ref, x1_ref, keep_ref, send_ref):
    z = pos_ref[1]
    h = jnp.concatenate(split((h0[...] + h1[...]) + (h2[...] + h3[...]), 3), 0)
    n = D // 8
    for i in range(N):
        part = z ^ BITS[i]
        columns = pl.ds(pl.multiple_of(part * n, n), n)
        x = jnp.concatenate([x0_ref[:, columns], x1_ref[:, columns]], 0)
        (keep_ref if i < 2 else send_ref)[i % 2] = add3(dot(h, x)) + (e0_ref[part] + e1_ref[part])


def sketch_part(pos, h, e, xs, after):
    return run(
        sketch_kernel,
        [shape((2, R, D // 8))] * 2,
        (pos, *h, *e, *xs),
        [SMEM] + [WHOLE] * 8,
        [WHOLE] * 2,
        after,
    )


def basis_kernel(pos_ref, mine_ref, other_ref, out_ref, s_ref):
    c, z = pos_ref[0], pos_ref[1]
    n = D // 8
    for half, ref in ((1 - c, mine_ref), (c, other_ref)):
        for i in range(N):
            chunk = half * N + (z ^ BITS[i])
            s_ref[:, pl.ds(pl.multiple_of(chunk * n, n), n)] = ref[i] * 0.25
    s = s_ref[...]
    gram = dot_both(s, s, NT)
    row = lax.broadcasted_iota(jnp.int32, (R, 2 * R), 0)
    col = lax.broadcasted_iota(jnp.int32, (R, 2 * R), 1)
    work = jnp.concatenate([gram, jnp.zeros((R, R), F32)], 1) + jnp.where(col == row + R, 1.0, 0.0)
    for j in range(R - 1):
        column = jnp.broadcast_to(work[:, j : j + 1], (R, 2 * R))
        line = work[j : j + 1, :] / column[j : j + 1, :]
        work = work - jnp.where(row > j, column, 0.0) * line
    pivot = jnp.sum(jnp.where(row == col, work, 0.0), 1, keepdims=True)
    done = work / jnp.sqrt(pivot)
    out_ref[...] = dot_both(done[:, R:], s, (((1,), (0,)), ((), ())))


def basis(pos, mine, other, after):
    return run(
        basis_kernel,
        pltpu.VMEM((R, D), F32),
        (pos, mine, other),
        [SMEM, WHOLE, WHOLE],
        WHOLE,
        after,
        scratch_shapes=[pltpu.VMEM((R, D), F32)],
    )


def block_rows(off_ref, g_ref, starts):
    rows = [pl.ds(pl.multiple_of(off_ref[start + k], T), T) for start in starts for k in range(4)]
    return jnp.concatenate([g_ref[at, :] for at in rows], 0)


def merge_kernel(starts, lo, hi, has_errors, has_acc, off_ref, pos_ref, g_ref, go_ref, *refs):
    n, step = len(starts), H // N
    xs, refs = refs[:n], list(refs[n:])
    e_ref = refs.pop(0) if has_errors else None
    own_in, other_in = (refs.pop(0), refs.pop(0)) if has_acc else (None, None)
    own_ref, other_ref = refs[:2]
    if has_errors:
        copies = fetches(e_ref, pos_ref[0], refs[2], refs[3], range(lo // step, hi // step))
        for copy in copies:
            copy.start()
    rows = jnp.concatenate([block_rows(off_ref, g_ref, starts), block_rows(off_ref, go_ref, starts)], 1)
    for k in range((hi - lo) // step):
        at = slice(lo + k * step, lo + (k + 1) * step)
        product = dot(jnp.concatenate([r[:, at] for r in xs], 0), rows, TN)
        if has_errors:
            copies[k].wait()
            own_ref[at, :] = refs[2][at, :] + product[:, :F]
            other_ref[at, :] = product[:, F:]
        else:
            own_ref[at, :] = own_in[at, :] + product[:, :F]
            other_ref[at, :] = other_in[at, :] + product[:, F:]


def merge(off, pos, g, g_other, groups, lo, hi, errors=None, acc=None, after=()):
    starts, xs = [start for start, _ in groups], [x for _, x in groups]
    args = [off, pos, g, g_other, *xs] + ([] if errors is None else [errors]) + ([] if acc is None else [*acc])
    specs = [SMEM] * 2 + [WHOLE] * (2 + len(xs)) + ([] if errors is None else [HBM]) + [WHOLE] * (2 if acc else 0)
    return run(
        functools.partial(merge_kernel, starts, lo, hi, errors is not None, acc is not None),
        [pltpu.VMEM((H, F), F32)] * 2,
        args,
        specs,
        [WHOLE] * 2,
        after,
        scratch_shapes=() if errors is None else FETCH,
        input_output_aliases={} if acc is None else {len(args) - 2: 0, len(args) - 1: 1},
    )


def last_other_kernel(starts, off_ref, acc_ref, g_ref, *refs):
    *xs, out_ref = refs
    rows, step = block_rows(off_ref, g_ref, starts), H // N
    for k in range(N):
        at = slice(k * step, (k + 1) * step)
        out_ref[at, :] = acc_ref[at, :] + dot(jnp.concatenate([r[:, at] for r in xs], 0), rows, TN)


def last_other(off, acc, groups, g, after):
    return run(
        functools.partial(last_other_kernel, [start for start, _ in groups]),
        pltpu.VMEM((H, F), F32),
        (off, acc, g, *[x for _, x in groups]),
        [SMEM] + [WHOLE] * (2 + len(groups)),
        WHOLE,
        after,
    )


def p_times(p, m):
    t1, t2 = split(m, 2)
    a, b = dot(p, t1), dot(p[: 2 * R], t2)
    return a[:R] + ((a[R : 2 * R] + b[:R]) + (a[2 * R :] + b[R:]))


def right_kernel(pos_ref, p_ref, own_ref, other_ref, e_ref, q_ref, send_ref, buf_ref, sems):
    copies = fetches(e_ref, 1 - pos_ref[0], buf_ref, sems)
    for copy in copies:
        copy.start()
    n = H // N
    q, send = jnp.zeros((R, F), F32), jnp.zeros((R, F), F32)
    for k in range(N):
        at = pl.ds(pl.multiple_of(pos_ref[0] * H + k * n, n), n)
        p = jnp.concatenate(split(p_ref[:, at], 3), 0)
        q += p_times(p, own_ref[k * n : (k + 1) * n, :])
        send += p_times(p, other_ref[k * n : (k + 1) * n, :])
    for k in range(N):
        at = pl.ds(pl.multiple_of((1 - pos_ref[0]) * H + k * n, n), n)
        p = jnp.concatenate(split(p_ref[:, at], 3), 0)
        copies[k].wait()
        q += p_times(p, buf_ref[k * n : (k + 1) * n, :])
    q_ref[...] = q
    send_ref[...] = send


def right_part(pos, p, acc, e, after):
    return run(
        right_kernel,
        [shape((R, F))] * 2 + [FETCH[0]],
        (pos, p, *acc, e),
        [SMEM] + [WHOLE] * 3 + [HBM],
        [WHOLE] * 3,
        after,
        scratch_shapes=FETCH[1:],
    )


def right_rest_kernel(starts, off_ref, pos_ref, p_ref, q_ref, send_ref, g_ref, go_ref, *refs):
    n = len(starts)
    xs, (out_ref, out_send_ref) = refs[:n], refs[n:]
    here = pl.ds(pl.multiple_of(pos_ref[0] * H, H), H)
    p = jnp.concatenate(split(p_ref[:, here], 3), 0)
    total, send = q_ref[...], send_ref[...]
    for start, x in zip(starts, xs):
        y = dot(x[...], p, NT)
        y = jnp.concatenate(split(y[:, :R] + (y[:, R : 2 * R] + y[:, 2 * R :]), 3), 1)
        rows = [pl.ds(pl.multiple_of(off_ref[start + k], T), T) for k in range(4)]
        total += add3(dot(y, jnp.concatenate([g_ref[at, :] for at in rows], 0), TN))
        send += add3(dot(y, jnp.concatenate([go_ref[at, :] for at in rows], 0), TN))
    out_ref[...] = total
    out_send_ref[...] = send


def right_rest(off, pos, p, q, send, g, g_other, groups):
    return run(
        functools.partial(right_rest_kernel, [start for start, _ in groups]),
        [shape((R, F))] * 2,
        (off, pos, p, q, send, g, g_other, *[x for _, x in groups]),
        [SMEM] * 2 + [WHOLE] * (5 + len(groups)),
        [WHOLE] * 2,
        vmem=24,
    )


def final_kernel(starts, pos_ref, off_ref, m_ref, e_ref, got_ref, g_ref, *refs):
    n, step = len(starts), H // N
    xs, refs = refs[:n], refs[n:]
    p_ref, q0, q1, q2, q3, out_ref, q_ref, made_ref, out_sems = refs
    c = pos_ref[0]
    q = ((q0[...] + q1[...]) + (q2[...] + q3[...])) * 0.25
    q_ref[...] = q
    s1, s2 = split(-q, 2)
    low = jnp.concatenate([s1, s2, s1], 0)
    rows = jnp.concatenate([block_rows(off_ref, g_ref, starts), low], 0)
    sent = []
    for k in range(2 * N):
        own, at = k < N, slice(k % N * step, (k % N + 1) * step)
        first = pl.multiple_of((c if own else 1 - c) * H + k % N * step, step)
        p1, p2 = split(p_ref[:, pl.ds(first, step)], 2)
        p = jnp.concatenate([p1, p1, p2], 0)
        here = made_ref.at[pl.ds(k * step, step), :]
        if own:
            here[...] = m_ref[at, :] + dot(jnp.concatenate([r[:, at] for r in xs] + [p], 0), rows, TN)
        else:
            here[...] = (e_ref[at, :] + got_ref[at, :]) + dot(p, low, TN)
        sent.append(pltpu.make_async_copy(here, out_ref.at[pl.ds(first, step), :], out_sems.at[k]))
        sent[-1].start()
    for copy in sent:
        copy.wait()


def final(off, pos, own, e, got, groups, g, p, q):
    n = len(groups)
    return run(
        functools.partial(final_kernel, [start for start, _ in groups]),
        [shape((D, F)), shape((R, F))],
        [pos, off, own, e, got, g] + [x for _, x in groups] + [p, *q],
        [SMEM, SMEM] + [WHOLE] * (n + 5 + N),
        [HBM, WHOLE],
        vmem=24,
        scratch_shapes=[pltpu.VMEM((D, F), F32), pltpu.SemaphoreType.DMA((2 * N,))],
    )


def later(array, behind):
    return lax.optimization_barrier((array, behind))[0]


def body(x, g, e, q_init):
    me = lax.axis_index("tensor")
    pos = jnp.stack([me % 2, lax.axis_index("dp")]).astype(jnp.int32)
    off = lax.dynamic_index_in_dim(jnp.asarray(block_tables()), me, 0, keepdims=False)
    e, q = pltpu.with_memory_space_constraint(e[0], pltpu.HBM), q_init.T

    mine, send = cut(pos, x)
    (x0,) = pack(stack_kernel, (mine, swap(send)), (2 * T,), ())
    a, b = hop(x0, True, 1), hop(x0, True, -1)
    g_other = swap(later(g, x0))
    own, other = tokens(off, q, g, (x0,))
    got = swap(other)
    g_other = held(g_other, (own,))
    h = add_parts(own, got, (g_other,))
    h = [h[0]] + [twin(v, False, bit) for v, bit in zip(h[1:], BITS[1:])]
    e_other = errors(pos, q, e, 1, (h[0],))
    top, bottom = pack(halves_kernel, (a, b), (T, T), (e_other, *h[1:]))
    c, d = hop(top, True, 1), hop(bottom, True, -1)

    (g0,) = pack(stack_kernel, (x0, a), (4 * T,), (top,))
    l0, r0 = hop(g0, False, 1), hop(g0, False, -1)
    e_got = swap(later(e_other, g0))
    e_own = errors(pos, q, e, 0, (g0,))
    (g1,) = pack(stack_kernel, (b, c, d), (4 * T,), (e_own,))
    l1, r1 = hop(g1, False, 1), hop(g1, False, -1)

    keep, send = sketch_part(pos, h, (e_own, e_got), (g0, g1), ())
    got = hop_z(send, 1)
    near = [(0, g0), (4, g1)]
    acc = merge(off, pos, g, g_other, near, 0, H // 2, e, None, (send,))
    keep, send = add_pair(keep, got, (acc[0],))
    got = hop_z(send, 2)
    acc = merge(off, pos, g, g_other, near, H // 2, H, e, acc, (send,))
    (s,) = add([keep], [got], (acc[0],))
    got = twin(s, True, 1)
    l0, r0 = later(l0, s), later(r0, s)
    o0 = hop(l0, False, 1)
    mid = [(8, l0), (16, r0)]
    acc = merge(off, pos, g, g_other, mid, 0, H // 2, None, acc, (s,))
    (s,) = add([s], [got], (acc[0],))
    got = twin(s, True, 2)
    acc = merge(off, pos, g, g_other, mid, H // 2, H, None, acc, (s,))
    (s,) = add([s], [got], (acc[0],))
    s = swap(s)
    (s,) = add([s], [twin(s, True, 1)], ())
    (s,) = add([s], [twin(s, True, 2)], ())
    got = hop_z(s, 2)
    l1, r1 = later(l1, s), later(r1, s)
    o1 = hop(r1, False, -1)
    far = [(12, l1), (20, r1)]
    acc = merge(off, pos, g, g_other, far, 0, H // 2, None, acc, (s,))
    pair = jnp.stack([later(s, acc[0]), got])
    got = hop_z(pair, 1)
    acc = merge(off, pos, g, g_other, far, H // 2, H, None, acc, (pair,))
    stack = jnp.concatenate([later(pair, acc[0]), got])
    p = basis(pos, stack, swap(stack), (acc[0],))

    last = [(24, later(o0, p)), (28, later(o1, p))]
    qp, q_send, e_rest = right_part(pos, p, acc, e, ())
    qp, q_send = right_rest(off, pos, p, qp, q_send, g, g_other, last)
    q_got = swap(q_send)
    out = last_other(off, acc[1], last, g_other, (q_send,))
    (qp,) = add([qp], [q_got], (out,))
    out = swap(later(out, qp))
    qs = (qp, around_z(qp, 2), around_z(qp, 1), around_z(qp, -1))
    err, qf = final(off, pos, acc[0], e_rest, out, last, g, p, qs)
    return err[None], p.T, qf.T


def solution(mesh):
    in_specs = (
        P(("dp", "tensor"), None),
        P("dp", "tensor"),
        P("dp", None, "tensor"),
        P("tensor", None),
    )
    out_specs = (P("dp", None, "tensor"), P(), P("tensor", None))
    return jax.shard_map(body, mesh=mesh, in_specs=in_specs, out_specs=out_specs, check_vma=False)
```

```python
import functools

import jax
import jax.numpy as jnp
import numpy as np
from jax import lax
from jax.experimental import pallas as pl
from jax.experimental.pallas import tpu as pltpu
from jax.sharding import PartitionSpec as P

F32, BF16 = jnp.float32, jnp.bfloat16
N, R, D, F, T = 4, 32, 4096, 512, 128
OFFSETS = (0, -1, 1, 2)
BITS = (0, 2, 1, 3)
MIB = 1024 * 1024
WHOLE = pl.BlockSpec(memory_space=pltpu.VMEM)
SMEM = pl.BlockSpec(memory_space=pltpu.SMEM)
HBM = pl.BlockSpec(memory_space=pltpu.HBM)
NT = (((1,), (1,)), ((), ()))
TN = (((0,), (0,)), ((), ()))


def flat(x, y, c):
    return ((x % N) * N + y % N) * 2 + c


def along(x, y, c, first, d):
    return flat(x + d, y, c) if (c == 0) == first else flat(x, y + d, c)


PLANE = [(x, y, c) for x in range(N) for y in range(N) for c in range(2)]


def hop(array, first, d):
    pairs = [(flat(*p), along(*p, first, d)) for p in PLANE]
    return lax.ppermute(array, "tensor", pairs)


def swap(array):
    return lax.ppermute(array, "tensor", [(i, i ^ 1) for i in range(2 * N * N)])


def hop_z(array, bit):
    return lax.ppermute(array, "dp", [(i, i ^ bit) for i in range(N)])


def around_z(array, d):
    return lax.ppermute(array, "dp", [(i, (i + d) % N) for i in range(N)])


def twin(array, first, bit):
    pairs = []
    for x, y, c in PLANE:
        to = (x ^ bit, y, c) if (c == 0) == first else (x, y ^ bit, c)
        pairs.append((flat(x, y, c), flat(*to)))
    return lax.ppermute(array, "tensor", pairs)


def block_tables():
    offsets = np.zeros((2 * N * N, 2, N, N, 2), np.int32)
    moved = np.zeros((2 * N * N, N * N * 2), np.int32)
    for x, y, c in PLANE:
        at = y if c == 0 else x
        for i in range(N):
            for j, first in enumerate(OFFSETS):
                for kind, second in enumerate((OFFSETS[i], (at ^ BITS[i]) - at)):
                    dx, dy = (first, second) if c == 0 else (second, first)
                    for m in range(2):
                        offsets[flat(x, y, c), kind, i, j, m] = flat(x + dx, y + dy, c ^ m) * T
    for x, y, c in PLANE:
        here = offsets[flat(x, y, c), 1].reshape(-1).tolist()
        there = offsets[flat(x, y, 1 - c), 1].reshape(-1).tolist()
        moved[flat(x, y, c)] = [here.index(row) for row in there]
    return np.concatenate([offsets.reshape(2 * N * N, -1), moved], 1)


def split(value, parts):
    pieces = []
    for _ in range(parts):
        piece = value.astype(BF16)
        pieces.append(piece)
        value = value - piece.astype(F32)
    return pieces


def dot(a, b, dims=(((1,), (0,)), ((), ()))):
    return lax.dot_general(a, b, dims, preferred_element_type=F32)


def dot_left(value, exact, dims):
    rows = value.shape[0]
    out = dot(jnp.concatenate(split(value, 3), 0), exact, dims)
    return out[:rows] + (out[rows : 2 * rows] + out[2 * rows :])


def dot_both(value, other, dims):
    rows = value.shape[0]
    a = jnp.concatenate(split(value, 3), 0)
    b1, b2, b3 = split(other, 3)
    p1, p2, p3 = dot(a, b1, dims), dot(a[: 2 * rows], b2, dims), dot(a[:rows], b3, dims)
    low = p1[2 * rows :] + p2[rows:] + p3
    return p1[:rows] + ((p1[rows : 2 * rows] + p2[:rows]) + low)


def shape(dims, dtype=F32):
    return jax.ShapeDtypeStruct(dims, dtype)


def run(kernel, out_shape, args, in_specs, out_specs, after=(), **kw):
    n, m = len(args), len(after)
    grid = kw.pop("grid", None)
    kw["cost_estimate"] = pl.CostEstimate(flops=1000, bytes_accessed=1000, transcendentals=0)
    prefetch = kw.pop("prefetch", 0)
    options = pltpu.CompilerParams(vmem_limit_bytes=kw.pop("vmem", 16) * MIB)
    any_spec = pl.BlockSpec(memory_space=pl.ANY)
    in_specs = list(in_specs) + [any_spec] * m

    def wrapped(*refs):
        kernel(*refs[:n], *refs[n + m :])

    if prefetch:
        kw["grid_spec"] = pltpu.PrefetchScalarGridSpec(
            num_scalar_prefetch=prefetch,
            grid=grid,
            in_specs=in_specs,
            out_specs=out_specs,
            scratch_shapes=kw.pop("scratch_shapes", ()),
        )
    else:
        kw.update(in_specs=in_specs, out_specs=out_specs)
        if grid is not None:
            kw["grid"] = grid
    return pl.pallas_call(wrapped, out_shape=out_shape, compiler_params=options, **kw)(*args, *after)


def add3(r):
    return r[:R] + (r[R : 2 * R] + r[2 * R :])


H = D // 2
B = 2 * N * N


def tokens_kernel(off_ref, q_ref, g_ref, own_ref, other_ref, h_ref):
    q = jnp.concatenate(split(q_ref[...], 3), 0)
    for k in range(N * 2):
        rows = [g_ref[pl.ds(pl.multiple_of(off_ref[B + k * N + j], T), T), :] for j in range(N)]
        r = add3(dot(q, jnp.concatenate(rows, 0), NT))
        for j in range(N):
            h_ref[k * N + j] = r[:, j * T : (j + 1) * T]
    for i in range(N):
        for k in range(2 * N):
            own_ref[i, :, k * T : (k + 1) * T] = h_ref[i * 2 * N + k]
            other_ref[i, :, k * T : (k + 1) * T] = h_ref[off_ref[2 * B + i * 2 * N + k]]


def tokens(off, q, g, after):
    w = 2 * N * T
    return run(
        tokens_kernel,
        [shape((N, R, w))] * 2,
        (off, q, g),
        [SMEM, WHOLE, WHOLE],
        [WHOLE] * 2,
        after,
        scratch_shapes=[pltpu.VMEM((B, R, T), F32)],
    )


def fetches(e_ref, half, buf_ref, sems, parts=range(N)):
    n = H // N
    return [
        pltpu.make_async_copy(
            e_ref.at[pl.ds(pl.multiple_of(half * H + k * n, n), n), :], buf_ref.at[pl.ds(k * n, n), :], sems.at[k]
        )
        for k in parts
    ]


FETCH = [pltpu.VMEM((H, F), F32), pltpu.SemaphoreType.DMA((N,))]


def errors_kernel(other, pos_ref, q_ref, e_ref, out_ref, buf_ref, sems):
    copies = fetches(e_ref, pos_ref[0] ^ other, buf_ref, sems)
    for copy in copies:
        copy.start()
    q = jnp.concatenate(split(q_ref[...], 3), 0)
    n = H // N
    for k in range(N):
        copies[k].wait()
        e1, e2 = split(buf_ref[k * n : (k + 1) * n, :], 2)
        r, s = dot(q, e1, NT), dot(q[: 2 * R], e2, NT)
        out_ref[k] = r[:R] + ((r[R : 2 * R] + s[:R]) + (r[2 * R :] + s[R:]))


def errors(pos, q, e, other, after):
    return run(
        functools.partial(errors_kernel, other),
        shape((N, R, D // 8)),
        (pos, q, e),
        [SMEM, WHOLE, HBM],
        WHOLE,
        after,
        scratch_shapes=FETCH,
    )


def add_kernel(n, *refs):
    for i in range(n):
        refs[2 * n + i][...] = refs[i][...] + refs[n + i][...]


def add(a, b, after=()):
    n = len(a)
    return run(
        functools.partial(add_kernel, n),
        [shape(v.shape) for v in a],
        (*a, *b),
        [WHOLE] * (2 * n),
        [WHOLE] * n,
        after,
    )


def add_parts_kernel(a_ref, b_ref, *outs):
    for i, out in enumerate(outs):
        out[...] = a_ref[i] + b_ref[i]


def add_parts(a, b, after=()):
    return run(add_parts_kernel, [shape(a.shape[1:])] * a.shape[0], (a, b), [WHOLE] * 2, [WHOLE] * a.shape[0], after)


def add_pair_kernel(a_ref, got_ref, keep_ref, send_ref):
    keep_ref[...] = a_ref[0] + got_ref[0]
    send_ref[...] = a_ref[1] + got_ref[1]


def add_pair(a, got, after=()):
    return run(
        add_pair_kernel,
        [shape(a.shape[1:])] * 2,
        (a, got),
        [WHOLE] * 2,
        [WHOLE] * 2,
        after,
    )


def cut_kernel(pos_ref, x_ref, mine_ref, send_ref):
    at = pl.multiple_of(pos_ref[0] * H, H)
    mine_ref[...] = x_ref[:, pl.ds(at, H)]
    send_ref[...] = x_ref[:, pl.ds(H - at, H)]


def cut(pos, x):
    return run(cut_kernel, [shape((T, H), BF16)] * 2, (pos, x), [SMEM, WHOLE], [WHOLE] * 2)


def halves_kernel(a, b, top, bottom):
    top[...] = a[:T, :]
    bottom[...] = b[T:, :]


def stack_kernel(*refs):
    *parts, out = refs
    at = 0
    for part in parts:
        out[at : at + part.shape[0], :] = part[...]
        at += part.shape[0]


def pack(kernel, args, rows, after):
    return run(kernel, [shape((r, H), BF16) for r in rows], args, [WHOLE] * len(args), [WHOLE] * len(rows), after)


def held_kernel(in_ref, out_ref):
    out_ref[...] = in_ref[...]


def held(array, after):
    return run(held_kernel, pltpu.VMEM(array.shape, array.dtype), (array,), [WHOLE], WHOLE, after)


def sketch_kernel(pos_ref, h0, h1, h2, h3, e0_ref, e1_ref, x0_ref, x1_ref, keep_ref, send_ref):
    z = pos_ref[1]
    h = jnp.concatenate(split((h0[...] + h1[...]) + (h2[...] + h3[...]), 3), 0)
    n = D // 8
    for i in range(N):
        part = z ^ BITS[i]
        columns = pl.ds(pl.multiple_of(part * n, n), n)
        x = jnp.concatenate([x0_ref[:, columns], x1_ref[:, columns]], 0)
        (keep_ref if i < 2 else send_ref)[i % 2] = add3(dot(h, x)) + (e0_ref[part] + e1_ref[part])


def sketch_part(pos, h, e, xs, after):
    return run(
        sketch_kernel,
        [shape((2, R, D // 8))] * 2,
        (pos, *h, *e, *xs),
        [SMEM] + [WHOLE] * 8,
        [WHOLE] * 2,
        after,
    )


def basis_kernel(pos_ref, mine_ref, other_ref, out_ref, s_ref):
    c, z = pos_ref[0], pos_ref[1]
    n = D // 8
    for half, ref in ((1 - c, mine_ref), (c, other_ref)):
        for i in range(N):
            chunk = half * N + (z ^ BITS[i])
            s_ref[:, pl.ds(pl.multiple_of(chunk * n, n), n)] = ref[i] * 0.25
    s = s_ref[...]
    gram = dot_both(s, s, NT)
    row = lax.broadcasted_iota(jnp.int32, (R, 2 * R), 0)
    col = lax.broadcasted_iota(jnp.int32, (R, 2 * R), 1)
    work = jnp.concatenate([gram, jnp.zeros((R, R), F32)], 1) + jnp.where(col == row + R, 1.0, 0.0)
    for j in range(R - 1):
        column = jnp.broadcast_to(work[:, j : j + 1], (R, 2 * R))
        line = work[j : j + 1, :] / column[j : j + 1, :]
        work = work - jnp.where(row > j, column, 0.0) * line
    pivot = jnp.sum(jnp.where(row == col, work, 0.0), 1, keepdims=True)
    done = work / jnp.sqrt(pivot)
    out_ref[...] = dot_both(done[:, R:], s, (((1,), (0,)), ((), ())))


def basis(pos, mine, other, after):
    return run(
        basis_kernel,
        pltpu.VMEM((R, D), F32),
        (pos, mine, other),
        [SMEM, WHOLE, WHOLE],
        WHOLE,
        after,
        scratch_shapes=[pltpu.VMEM((R, D), F32)],
    )


def block_rows(off_ref, g_ref, starts):
    rows = [pl.ds(pl.multiple_of(off_ref[start + k], T), T) for start in starts for k in range(4)]
    return jnp.concatenate([g_ref[at, :] for at in rows], 0)


def merge_kernel(starts, lo, hi, has_errors, has_acc, off_ref, pos_ref, g_ref, go_ref, *refs):
    n, step = len(starts), H // N
    xs, refs = refs[:n], list(refs[n:])
    e_ref = refs.pop(0) if has_errors else None
    own_in, other_in = (refs.pop(0), refs.pop(0)) if has_acc else (None, None)
    own_ref, other_ref = refs[:2]
    if has_errors:
        copies = fetches(e_ref, pos_ref[0], refs[2], refs[3], range(lo // step, hi // step))
        for copy in copies:
            copy.start()
    rows = jnp.concatenate([block_rows(off_ref, g_ref, starts), block_rows(off_ref, go_ref, starts)], 1)
    for k in range((hi - lo) // step):
        at = slice(lo + k * step, lo + (k + 1) * step)
        product = dot(jnp.concatenate([r[:, at] for r in xs], 0), rows, TN)
        if has_errors:
            copies[k].wait()
            own_ref[at, :] = refs[2][at, :] + product[:, :F]
            other_ref[at, :] = product[:, F:]
        else:
            own_ref[at, :] = own_in[at, :] + product[:, :F]
            other_ref[at, :] = other_in[at, :] + product[:, F:]


def merge(off, pos, g, g_other, groups, lo, hi, errors=None, acc=None, after=()):
    starts, xs = [start for start, _ in groups], [x for _, x in groups]
    args = [off, pos, g, g_other, *xs] + ([] if errors is None else [errors]) + ([] if acc is None else [*acc])
    specs = [SMEM] * 2 + [WHOLE] * (2 + len(xs)) + ([] if errors is None else [HBM]) + [WHOLE] * (2 if acc else 0)
    return run(
        functools.partial(merge_kernel, starts, lo, hi, errors is not None, acc is not None),
        [pltpu.VMEM((H, F), F32)] * 2,
        args,
        specs,
        [WHOLE] * 2,
        after,
        scratch_shapes=() if errors is None else FETCH,
        input_output_aliases={} if acc is None else {len(args) - 2: 0, len(args) - 1: 1},
    )


def last_other_kernel(starts, off_ref, acc_ref, g_ref, *refs):
    *xs, out_ref = refs
    rows, step = block_rows(off_ref, g_ref, starts), H // N
    for k in range(N):
        at = slice(k * step, (k + 1) * step)
        out_ref[at, :] = acc_ref[at, :] + dot(jnp.concatenate([r[:, at] for r in xs], 0), rows, TN)


def last_other(off, acc, groups, g, after):
    return run(
        functools.partial(last_other_kernel, [start for start, _ in groups]),
        pltpu.VMEM((H, F), F32),
        (off, acc, g, *[x for _, x in groups]),
        [SMEM] + [WHOLE] * (2 + len(groups)),
        WHOLE,
        after,
    )


def p_times(p, m):
    t1, t2 = split(m, 2)
    a, b = dot(p, t1), dot(p[: 2 * R], t2)
    return a[:R] + ((a[R : 2 * R] + b[:R]) + (a[2 * R :] + b[R:]))


def right_kernel(pos_ref, p_ref, own_ref, other_ref, e_ref, q_ref, send_ref, buf_ref, sems):
    copies = fetches(e_ref, 1 - pos_ref[0], buf_ref, sems)
    for copy in copies:
        copy.start()
    n = H // N
    q, send = jnp.zeros((R, F), F32), jnp.zeros((R, F), F32)
    for k in range(N):
        at = pl.ds(pl.multiple_of(pos_ref[0] * H + k * n, n), n)
        p = jnp.concatenate(split(p_ref[:, at], 3), 0)
        q += p_times(p, own_ref[k * n : (k + 1) * n, :])
        send += p_times(p, other_ref[k * n : (k + 1) * n, :])
    for k in range(N):
        at = pl.ds(pl.multiple_of((1 - pos_ref[0]) * H + k * n, n), n)
        p = jnp.concatenate(split(p_ref[:, at], 3), 0)
        copies[k].wait()
        q += p_times(p, buf_ref[k * n : (k + 1) * n, :])
    q_ref[...] = q
    send_ref[...] = send


def right_part(pos, p, acc, e, after):
    return run(
        right_kernel,
        [shape((R, F))] * 2 + [FETCH[0]],
        (pos, p, *acc, e),
        [SMEM] + [WHOLE] * 3 + [HBM],
        [WHOLE] * 3,
        after,
        scratch_shapes=FETCH[1:],
    )


def right_rest_kernel(starts, off_ref, pos_ref, p_ref, q_ref, send_ref, g_ref, go_ref, *refs):
    n = len(starts)
    xs, (out_ref, out_send_ref) = refs[:n], refs[n:]
    here = pl.ds(pl.multiple_of(pos_ref[0] * H, H), H)
    p = jnp.concatenate(split(p_ref[:, here], 3), 0)
    total, send = q_ref[...], send_ref[...]
    for start, x in zip(starts, xs):
        y = dot(x[...], p, NT)
        y = jnp.concatenate(split(y[:, :R] + (y[:, R : 2 * R] + y[:, 2 * R :]), 3), 1)
        rows = [pl.ds(pl.multiple_of(off_ref[start + k], T), T) for k in range(4)]
        total += add3(dot(y, jnp.concatenate([g_ref[at, :] for at in rows], 0), TN))
        send += add3(dot(y, jnp.concatenate([go_ref[at, :] for at in rows], 0), TN))
    out_ref[...] = total
    out_send_ref[...] = send


def right_rest(off, pos, p, q, send, g, g_other, groups):
    return run(
        functools.partial(right_rest_kernel, [start for start, _ in groups]),
        [shape((R, F))] * 2,
        (off, pos, p, q, send, g, g_other, *[x for _, x in groups]),
        [SMEM] * 2 + [WHOLE] * (5 + len(groups)),
        [WHOLE] * 2,
        vmem=24,
    )


def final_kernel(starts, pos_ref, off_ref, m_ref, e_ref, got_ref, g_ref, *refs):
    n, step = len(starts), H // N
    xs, refs = refs[:n], refs[n:]
    p_ref, q0, q1, q2, q3, out_ref, q_ref, p_out_ref, made_ref, out_sems = refs
    c = pos_ref[0]
    q = ((q0[...] + q1[...]) + (q2[...] + q3[...])) * 0.25
    q_ref[...] = q
    s1, s2 = split(-q, 2)
    low = jnp.concatenate([s1, s2, s1], 0)
    rows = jnp.concatenate([block_rows(off_ref, g_ref, starts), low], 0)
    sent = [pltpu.make_async_copy(p_ref, p_out_ref, out_sems.at[2 * N])]
    sent[0].start()
    for k in range(2 * N):
        own, at = k < N, slice(k % N * step, (k % N + 1) * step)
        first = pl.multiple_of((c if own else 1 - c) * H + k % N * step, step)
        p1, p2 = split(p_ref[:, pl.ds(first, step)], 2)
        p = jnp.concatenate([p1, p1, p2], 0)
        here = made_ref.at[pl.ds(k * step, step), :]
        if own:
            here[...] = m_ref[at, :] + dot(jnp.concatenate([r[:, at] for r in xs] + [p], 0), rows, TN)
        else:
            here[...] = (e_ref[at, :] + got_ref[at, :]) + dot(p, low, TN)
        sent.append(pltpu.make_async_copy(here, out_ref.at[pl.ds(first, step), :], out_sems.at[k]))
        sent[-1].start()
    for copy in sent:
        copy.wait()


def final(off, pos, own, e, got, groups, g, p, q):
    n = len(groups)
    return run(
        functools.partial(final_kernel, [start for start, _ in groups]),
        [shape((D, F)), shape((R, F)), shape((R, D))],
        [pos, off, own, e, got, g] + [x for _, x in groups] + [p, *q],
        [SMEM, SMEM] + [WHOLE] * (n + 5 + N),
        [HBM, WHOLE, HBM],
        vmem=24,
        scratch_shapes=[pltpu.VMEM((D, F), F32), pltpu.SemaphoreType.DMA((2 * N + 1,))],
    )


def later(array, behind):
    return lax.optimization_barrier((array, behind))[0]


def body(x, g, e, q_init):
    me = lax.axis_index("tensor")
    pos = jnp.stack([me % 2, lax.axis_index("dp")]).astype(jnp.int32)
    off = lax.dynamic_index_in_dim(jnp.asarray(block_tables()), me, 0, keepdims=False)
    e, q = pltpu.with_memory_space_constraint(e[0], pltpu.HBM), q_init.T

    mine, send = cut(pos, x)
    (x0,) = pack(stack_kernel, (mine, swap(send)), (2 * T,), ())
    a, b = hop(x0, True, 1), hop(x0, True, -1)
    g_other = swap(later(g, x0))
    own, other = tokens(off, q, g, (x0,))
    got = swap(other)
    g_other = held(g_other, (own,))
    h = add_parts(own, got, (g_other,))
    h = [h[0]] + [twin(v, False, bit) for v, bit in zip(h[1:], BITS[1:])]
    e_other = errors(pos, q, e, 1, (h[0],))
    top, bottom = pack(halves_kernel, (a, b), (T, T), (e_other, *h[1:]))
    c, d = hop(top, True, 1), hop(bottom, True, -1)

    (g0,) = pack(stack_kernel, (x0, a), (4 * T,), (top,))
    l0, r0 = hop(g0, False, 1), hop(g0, False, -1)
    e_got = swap(later(e_other, g0))
    e_own = errors(pos, q, e, 0, (g0,))
    (g1,) = pack(stack_kernel, (b, c, d), (4 * T,), (e_own,))
    l1, r1 = hop(g1, False, 1), hop(g1, False, -1)

    keep, send = sketch_part(pos, h, (e_own, e_got), (g0, g1), ())
    got = hop_z(send, 1)
    near = [(0, g0), (4, g1)]
    acc = merge(off, pos, g, g_other, near, 0, H // 2, e, None, (send,))
    keep, send = add_pair(keep, got, (acc[0],))
    got = hop_z(send, 2)
    acc = merge(off, pos, g, g_other, near, H // 2, H, e, acc, (send,))
    (s,) = add([keep], [got], (acc[0],))
    got = twin(s, True, 1)
    l0, r0 = later(l0, s), later(r0, s)
    o0 = hop(l0, False, 1)
    mid = [(8, l0), (16, r0)]
    acc = merge(off, pos, g, g_other, mid, 0, H // 2, None, acc, (s,))
    (s,) = add([s], [got], (acc[0],))
    got = twin(s, True, 2)
    acc = merge(off, pos, g, g_other, mid, H // 2, H, None, acc, (s,))
    (s,) = add([s], [got], (acc[0],))
    s = swap(s)
    (s,) = add([s], [twin(s, True, 1)], ())
    (s,) = add([s], [twin(s, True, 2)], ())
    got = hop_z(s, 2)
    l1, r1 = later(l1, s), later(r1, s)
    o1 = hop(r1, False, -1)
    far = [(12, l1), (20, r1)]
    acc = merge(off, pos, g, g_other, far, 0, H // 2, None, acc, (s,))
    pair = jnp.stack([later(s, acc[0]), got])
    got = hop_z(pair, 1)
    acc = merge(off, pos, g, g_other, far, H // 2, H, None, acc, (pair,))
    stack = jnp.concatenate([later(pair, acc[0]), got])
    p = basis(pos, stack, swap(stack), (acc[0],))

    o0 = later(o0, p)
    qp, q_send, e_rest = right_part(pos, p, acc, e, ())
    qp, q_send = right_rest(off, pos, p, qp, q_send, g, g_other, [(24, o0)])
    o1 = later(o1, qp)
    last = [(24, o0), (28, o1)]
    qp, q_send = right_rest(off, pos, p, qp, q_send, g, g_other, last[1:])
    q_got = swap(q_send)
    out = last_other(off, acc[1], last, g_other, (q_send,))
    (qp,) = add([qp], [q_got], (out,))
    out = swap(later(out, qp))
    qs = (qp, around_z(qp, 2), around_z(qp, 1), around_z(qp, -1))
    err, qf, pf = final(off, pos, acc[0], e_rest, out, last, g, p, qs)
    return err[None], pf.T, qf.T


def solution(mesh):
    in_specs = (
        P(("dp", "tensor"), None),
        P("dp", "tensor"),
        P("dp", None, "tensor"),
        P("tensor", None),
    )
    out_specs = (P("dp", None, "tensor"), P(), P("tensor", None))
    return jax.shard_map(body, mesh=mesh, in_specs=in_specs, out_specs=out_specs, check_vma=False)
```

```python
import functools

import jax
import jax.numpy as jnp
import numpy as np
from jax import lax
from jax.experimental import pallas as pl
from jax.experimental.pallas import tpu as pltpu
from jax.sharding import PartitionSpec as P

F32, BF16 = jnp.float32, jnp.bfloat16
N, R, D, F, T = 4, 32, 4096, 512, 128
OFFSETS = (0, -1, 1, 2)
BITS = (0, 2, 1, 3)
MIB = 1024 * 1024
WHOLE = pl.BlockSpec(memory_space=pltpu.VMEM)
SMEM = pl.BlockSpec(memory_space=pltpu.SMEM)
HBM = pl.BlockSpec(memory_space=pltpu.HBM)
NT = (((1,), (1,)), ((), ()))
TN = (((0,), (0,)), ((), ()))


def flat(x, y, c):
    return ((x % N) * N + y % N) * 2 + c


def along(x, y, c, first, d):
    return flat(x + d, y, c) if (c == 0) == first else flat(x, y + d, c)


PLANE = [(x, y, c) for x in range(N) for y in range(N) for c in range(2)]


def hop(array, first, d):
    pairs = [(flat(*p), along(*p, first, d)) for p in PLANE]
    return lax.ppermute(array, "tensor", pairs)


def swap(array):
    return lax.ppermute(array, "tensor", [(i, i ^ 1) for i in range(2 * N * N)])


def hop_z(array, bit):
    return lax.ppermute(array, "dp", [(i, i ^ bit) for i in range(N)])


def around_z(array, d):
    return lax.ppermute(array, "dp", [(i, (i + d) % N) for i in range(N)])


def twin(array, first, bit):
    pairs = []
    for x, y, c in PLANE:
        to = (x ^ bit, y, c) if (c == 0) == first else (x, y ^ bit, c)
        pairs.append((flat(x, y, c), flat(*to)))
    return lax.ppermute(array, "tensor", pairs)


def block_tables():
    offsets = np.zeros((2 * N * N, 2, N, N, 2), np.int32)
    moved = np.zeros((2 * N * N, N * N * 2), np.int32)
    for x, y, c in PLANE:
        at = y if c == 0 else x
        for i in range(N):
            for j, first in enumerate(OFFSETS):
                for kind, second in enumerate((OFFSETS[i], (at ^ BITS[i]) - at)):
                    dx, dy = (first, second) if c == 0 else (second, first)
                    for m in range(2):
                        offsets[flat(x, y, c), kind, i, j, m] = flat(x + dx, y + dy, c ^ m) * T
    for x, y, c in PLANE:
        here = offsets[flat(x, y, c), 1].reshape(-1).tolist()
        there = offsets[flat(x, y, 1 - c), 1].reshape(-1).tolist()
        moved[flat(x, y, c)] = [here.index(row) for row in there]
    return np.concatenate([offsets.reshape(2 * N * N, -1), moved], 1)


def split(value, parts):
    pieces = []
    for _ in range(parts):
        piece = value.astype(BF16)
        pieces.append(piece)
        value = value - piece.astype(F32)
    return pieces


def dot(a, b, dims=(((1,), (0,)), ((), ()))):
    return lax.dot_general(a, b, dims, preferred_element_type=F32)


def dot_left(value, exact, dims):
    rows = value.shape[0]
    out = dot(jnp.concatenate(split(value, 3), 0), exact, dims)
    return out[:rows] + (out[rows : 2 * rows] + out[2 * rows :])


def dot_both(value, other, dims):
    rows = value.shape[0]
    a = jnp.concatenate(split(value, 3), 0)
    b1, b2, b3 = split(other, 3)
    p1, p2, p3 = dot(a, b1, dims), dot(a[: 2 * rows], b2, dims), dot(a[:rows], b3, dims)
    low = p1[2 * rows :] + p2[rows:] + p3
    return p1[:rows] + ((p1[rows : 2 * rows] + p2[:rows]) + low)


def shape(dims, dtype=F32):
    return jax.ShapeDtypeStruct(dims, dtype)


def run(kernel, out_shape, args, in_specs, out_specs, after=(), **kw):
    n, m = len(args), len(after)
    grid = kw.pop("grid", None)
    kw["cost_estimate"] = pl.CostEstimate(flops=1000, bytes_accessed=1000, transcendentals=0)
    prefetch = kw.pop("prefetch", 0)
    options = pltpu.CompilerParams(vmem_limit_bytes=kw.pop("vmem", 16) * MIB)
    any_spec = pl.BlockSpec(memory_space=pl.ANY)
    in_specs = list(in_specs) + [any_spec] * m

    def wrapped(*refs):
        kernel(*refs[:n], *refs[n + m :])

    if prefetch:
        kw["grid_spec"] = pltpu.PrefetchScalarGridSpec(
            num_scalar_prefetch=prefetch,
            grid=grid,
            in_specs=in_specs,
            out_specs=out_specs,
            scratch_shapes=kw.pop("scratch_shapes", ()),
        )
    else:
        kw.update(in_specs=in_specs, out_specs=out_specs)
        if grid is not None:
            kw["grid"] = grid
    return pl.pallas_call(wrapped, out_shape=out_shape, compiler_params=options, **kw)(*args, *after)


def add3(r):
    return r[:R] + (r[R : 2 * R] + r[2 * R :])


H = D // 2
B = 2 * N * N


def tokens_kernel(off_ref, q_ref, g_ref, own_ref, other_ref, h_ref):
    q = jnp.concatenate(split(q_ref[...], 3), 0)
    for k in range(N * 2):
        rows = [g_ref[pl.ds(pl.multiple_of(off_ref[B + k * N + j], T), T), :] for j in range(N)]
        r = add3(dot(q, jnp.concatenate(rows, 0), NT))
        for j in range(N):
            h_ref[k * N + j] = r[:, j * T : (j + 1) * T]
    for i in range(N):
        for k in range(2 * N):
            own_ref[i, :, k * T : (k + 1) * T] = h_ref[i * 2 * N + k]
            other_ref[i, :, k * T : (k + 1) * T] = h_ref[off_ref[2 * B + i * 2 * N + k]]


def tokens(off, q, g, after):
    w = 2 * N * T
    return run(
        tokens_kernel,
        [shape((N, R, w))] * 2,
        (off, q, g),
        [SMEM, WHOLE, WHOLE],
        [WHOLE] * 2,
        after,
        scratch_shapes=[pltpu.VMEM((B, R, T), F32)],
    )


def fetches(e_ref, half, buf_ref, sems, parts=range(N)):
    n = H // N
    return [
        pltpu.make_async_copy(
            e_ref.at[pl.ds(pl.multiple_of(half * H + k * n, n), n), :], buf_ref.at[pl.ds(k * n, n), :], sems.at[k]
        )
        for k in parts
    ]


FETCH = [pltpu.VMEM((H, F), F32), pltpu.SemaphoreType.DMA((N,))]


def errors_kernel(other, pos_ref, q_ref, e_ref, out_ref, buf_ref, sems):
    copies = fetches(e_ref, pos_ref[0] ^ other, buf_ref, sems)
    for copy in copies:
        copy.start()
    q = jnp.concatenate(split(q_ref[...], 3), 0)
    n = H // N
    for k in range(N):
        copies[k].wait()
        e1, e2 = split(buf_ref[k * n : (k + 1) * n, :], 2)
        r, s = dot(q, e1, NT), dot(q[: 2 * R], e2, NT)
        out_ref[k] = r[:R] + ((r[R : 2 * R] + s[:R]) + (r[2 * R :] + s[R:]))


def errors(pos, q, e, other, after):
    return run(
        functools.partial(errors_kernel, other),
        shape((N, R, D // 8)),
        (pos, q, e),
        [SMEM, WHOLE, HBM],
        WHOLE,
        after,
        scratch_shapes=FETCH,
    )


def add_kernel(n, *refs):
    for i in range(n):
        refs[2 * n + i][...] = refs[i][...] + refs[n + i][...]


def add(a, b, after=()):
    n = len(a)
    return run(
        functools.partial(add_kernel, n),
        [shape(v.shape) for v in a],
        (*a, *b),
        [WHOLE] * (2 * n),
        [WHOLE] * n,
        after,
    )


def add_parts_kernel(a_ref, b_ref, *outs):
    for i, out in enumerate(outs):
        out[...] = a_ref[i] + b_ref[i]


def add_parts(a, b, after=()):
    return run(add_parts_kernel, [shape(a.shape[1:])] * a.shape[0], (a, b), [WHOLE] * 2, [WHOLE] * a.shape[0], after)


def add_pair_kernel(a_ref, got_ref, keep_ref, send_ref):
    keep_ref[...] = a_ref[0] + got_ref[0]
    send_ref[...] = a_ref[1] + got_ref[1]


def add_pair(a, got, after=()):
    return run(
        add_pair_kernel,
        [shape(a.shape[1:])] * 2,
        (a, got),
        [WHOLE] * 2,
        [WHOLE] * 2,
        after,
    )


def cut_kernel(pos_ref, x_ref, mine_ref, send_ref):
    at = pl.multiple_of(pos_ref[0] * H, H)
    mine_ref[...] = x_ref[:, pl.ds(at, H)]
    send_ref[...] = x_ref[:, pl.ds(H - at, H)]


def cut(pos, x):
    return run(cut_kernel, [shape((T, H), BF16)] * 2, (pos, x), [SMEM, WHOLE], [WHOLE] * 2)


def halves_kernel(a, b, top, bottom):
    top[...] = a[:T, :]
    bottom[...] = b[T:, :]


def stack_kernel(*refs):
    *parts, out = refs
    at = 0
    for part in parts:
        out[at : at + part.shape[0], :] = part[...]
        at += part.shape[0]


def pack(kernel, args, rows, after):
    return run(kernel, [shape((r, H), BF16) for r in rows], args, [WHOLE] * len(args), [WHOLE] * len(rows), after)


def held_kernel(in_ref, out_ref):
    out_ref[...] = in_ref[...]


def held(array, after):
    return run(held_kernel, pltpu.VMEM(array.shape, array.dtype), (array,), [WHOLE], WHOLE, after)


def sketch_kernel(pos_ref, h0, h1, h2, h3, e0_ref, e1_ref, x0_ref, x1_ref, keep_ref, send_ref):
    z = pos_ref[1]
    h = jnp.concatenate(split((h0[...] + h1[...]) + (h2[...] + h3[...]), 3), 0)
    n = D // 8
    for i in range(N):
        part = z ^ BITS[i]
        columns = pl.ds(pl.multiple_of(part * n, n), n)
        x = jnp.concatenate([x0_ref[:, columns], x1_ref[:, columns]], 0)
        (keep_ref if i < 2 else send_ref)[i % 2] = add3(dot(h, x)) + (e0_ref[part] + e1_ref[part])


def sketch_part(pos, h, e, xs, after):
    return run(
        sketch_kernel,
        [shape((2, R, D // 8))] * 2,
        (pos, *h, *e, *xs),
        [SMEM] + [WHOLE] * 8,
        [WHOLE] * 2,
        after,
    )


def basis_kernel(pos_ref, mine_ref, other_ref, out_ref, s_ref):
    c, z = pos_ref[0], pos_ref[1]
    n = D // 8
    for half, ref in ((1 - c, mine_ref), (c, other_ref)):
        for i in range(N):
            chunk = half * N + (z ^ BITS[i])
            s_ref[:, pl.ds(pl.multiple_of(chunk * n, n), n)] = ref[i] * 0.25
    s = s_ref[...]
    gram = dot_both(s, s, NT)
    row = lax.broadcasted_iota(jnp.int32, (R, 2 * R), 0)
    col = lax.broadcasted_iota(jnp.int32, (R, 2 * R), 1)
    work = jnp.concatenate([gram, jnp.zeros((R, R), F32)], 1) + jnp.where(col == row + R, 1.0, 0.0)
    for j in range(R - 1):
        column = jnp.broadcast_to(work[:, j : j + 1], (R, 2 * R))
        line = work[j : j + 1, :] / column[j : j + 1, :]
        work = work - jnp.where(row > j, column, 0.0) * line
    pivot = jnp.sum(jnp.where(row == col, work, 0.0), 1, keepdims=True)
    done = work / jnp.sqrt(pivot)
    out_ref[...] = dot_both(done[:, R:], s, (((1,), (0,)), ((), ())))


def basis(pos, mine, other, after):
    return run(
        basis_kernel,
        pltpu.VMEM((R, D), F32),
        (pos, mine, other),
        [SMEM, WHOLE, WHOLE],
        WHOLE,
        after,
        scratch_shapes=[pltpu.VMEM((R, D), F32)],
    )


def block_rows(off_ref, g_ref, starts):
    rows = [pl.ds(pl.multiple_of(off_ref[start + k], T), T) for start in starts for k in range(4)]
    return jnp.concatenate([g_ref[at, :] for at in rows], 0)


def merge_kernel(starts, lo, hi, has_errors, has_acc, off_ref, pos_ref, g_ref, go_ref, *refs):
    n, step = len(starts), H // N
    xs, refs = refs[:n], list(refs[n:])
    e_ref = refs.pop(0) if has_errors else None
    own_in, other_in = (refs.pop(0), refs.pop(0)) if has_acc else (None, None)
    own_ref, other_ref = refs[:2]
    if has_errors:
        copies = fetches(e_ref, pos_ref[0], refs[2], refs[3], range(lo // step, hi // step))
        for copy in copies:
            copy.start()
    rows = jnp.concatenate([block_rows(off_ref, g_ref, starts), block_rows(off_ref, go_ref, starts)], 1)
    for k in range((hi - lo) // step):
        at = slice(lo + k * step, lo + (k + 1) * step)
        product = dot(jnp.concatenate([r[:, at] for r in xs], 0), rows, TN)
        if has_errors:
            copies[k].wait()
            own_ref[at, :] = refs[2][at, :] + product[:, :F]
            other_ref[at, :] = product[:, F:]
        else:
            own_ref[at, :] = own_in[at, :] + product[:, :F]
            other_ref[at, :] = other_in[at, :] + product[:, F:]


def merge(off, pos, g, g_other, groups, lo, hi, errors=None, acc=None, after=()):
    starts, xs = [start for start, _ in groups], [x for _, x in groups]
    args = [off, pos, g, g_other, *xs] + ([] if errors is None else [errors]) + ([] if acc is None else [*acc])
    specs = [SMEM] * 2 + [WHOLE] * (2 + len(xs)) + ([] if errors is None else [HBM]) + [WHOLE] * (2 if acc else 0)
    return run(
        functools.partial(merge_kernel, starts, lo, hi, errors is not None, acc is not None),
        [pltpu.VMEM((H, F), F32)] * 2,
        args,
        specs,
        [WHOLE] * 2,
        after,
        scratch_shapes=() if errors is None else FETCH,
        input_output_aliases={} if acc is None else {len(args) - 2: 0, len(args) - 1: 1},
    )


def last_other_kernel(starts, off_ref, acc_ref, g_ref, *refs):
    *xs, out_ref = refs
    rows, step = block_rows(off_ref, g_ref, starts), H // N
    for k in range(N):
        at = slice(k * step, (k + 1) * step)
        out_ref[at, :] = acc_ref[at, :] + dot(jnp.concatenate([r[:, at] for r in xs], 0), rows, TN)


def last_other(off, acc, groups, g, after):
    return run(
        functools.partial(last_other_kernel, [start for start, _ in groups]),
        pltpu.VMEM((H, F), F32),
        (off, acc, g, *[x for _, x in groups]),
        [SMEM] + [WHOLE] * (2 + len(groups)),
        WHOLE,
        after,
    )


def p_times(p, m):
    t1, t2 = split(m, 2)
    a, b = dot(p, t1), dot(p[: 2 * R], t2)
    return a[:R] + ((a[R : 2 * R] + b[:R]) + (a[2 * R :] + b[R:]))


def right_kernel(pos_ref, p_ref, own_ref, other_ref, e_ref, q_ref, send_ref, buf_ref, sems):
    copies = fetches(e_ref, 1 - pos_ref[0], buf_ref, sems)
    for copy in copies:
        copy.start()
    n = H // N
    q, send = jnp.zeros((R, F), F32), jnp.zeros((R, F), F32)
    for k in range(N):
        at = pl.ds(pl.multiple_of(pos_ref[0] * H + k * n, n), n)
        p = jnp.concatenate(split(p_ref[:, at], 3), 0)
        q += p_times(p, own_ref[k * n : (k + 1) * n, :])
        send += p_times(p, other_ref[k * n : (k + 1) * n, :])
    for k in range(N):
        at = pl.ds(pl.multiple_of((1 - pos_ref[0]) * H + k * n, n), n)
        p = jnp.concatenate(split(p_ref[:, at], 3), 0)
        copies[k].wait()
        q += p_times(p, buf_ref[k * n : (k + 1) * n, :])
    q_ref[...] = q
    send_ref[...] = send


def right_part(pos, p, acc, e, after):
    return run(
        right_kernel,
        [shape((R, F))] * 2 + [FETCH[0]],
        (pos, p, *acc, e),
        [SMEM] + [WHOLE] * 3 + [HBM],
        [WHOLE] * 3,
        after,
        scratch_shapes=FETCH[1:],
    )


def right_rest_kernel(starts, off_ref, pos_ref, p_ref, q_ref, send_ref, g_ref, go_ref, *refs):
    n = len(starts)
    xs, (out_ref, out_send_ref) = refs[:n], refs[n:]
    here = pl.ds(pl.multiple_of(pos_ref[0] * H, H), H)
    p = jnp.concatenate(split(p_ref[:, here], 3), 0)
    total, send = q_ref[...], send_ref[...]
    for start, x in zip(starts, xs):
        y = dot(x[...], p, NT)
        y = jnp.concatenate(split(y[:, :R] + (y[:, R : 2 * R] + y[:, 2 * R :]), 3), 1)
        rows = [pl.ds(pl.multiple_of(off_ref[start + k], T), T) for k in range(4)]
        total += add3(dot(y, jnp.concatenate([g_ref[at, :] for at in rows], 0), TN))
        send += add3(dot(y, jnp.concatenate([go_ref[at, :] for at in rows], 0), TN))
    out_ref[...] = total
    out_send_ref[...] = send


def right_rest(off, pos, p, q, send, g, g_other, groups):
    return run(
        functools.partial(right_rest_kernel, [start for start, _ in groups]),
        [shape((R, F))] * 2,
        (off, pos, p, q, send, g, g_other, *[x for _, x in groups]),
        [SMEM] * 2 + [WHOLE] * (5 + len(groups)),
        [WHOLE] * 2,
        vmem=24,
    )


def final_kernel(starts, pos_ref, off_ref, m_ref, e_ref, got_ref, g_ref, *refs):
    n, step = len(starts), H // N
    xs, refs = refs[:n], refs[n:]
    p_ref, q0, q1, q2, q3, out_ref, q_ref, p_out_ref, made_ref, out_sems = refs
    c = pos_ref[0]
    q = ((q0[...] + q1[...]) + (q2[...] + q3[...])) * 0.25
    q_ref[...] = q
    s1, s2 = split(-q, 2)
    low = jnp.concatenate([s1, s2, s1], 0)
    rows = jnp.concatenate([block_rows(off_ref, g_ref, starts), low], 0)
    sent = [pltpu.make_async_copy(p_ref, p_out_ref, out_sems.at[2 * N])]
    sent[0].start()
    for k in range(2 * N):
        own, at = k < N, slice(k % N * step, (k % N + 1) * step)
        first = pl.multiple_of((c if own else 1 - c) * H + k % N * step, step)
        p1, p2 = split(p_ref[:, pl.ds(first, step)], 2)
        p = jnp.concatenate([p1, p1, p2], 0)
        here = made_ref.at[pl.ds(k * step, step), :]
        if own:
            here[...] = m_ref[at, :] + dot(jnp.concatenate([r[:, at] for r in xs] + [p], 0), rows, TN)
        else:
            here[...] = (e_ref[at, :] + got_ref[at, :]) + dot(p, low, TN)
        sent.append(pltpu.make_async_copy(here, out_ref.at[pl.ds(first, step), :], out_sems.at[k]))
        sent[-1].start()
    for copy in sent:
        copy.wait()


def final(off, pos, own, e, got, groups, g, p, q):
    n = len(groups)
    return run(
        functools.partial(final_kernel, [start for start, _ in groups]),
        [shape((D, F)), shape((R, F)), shape((R, D))],
        [pos, off, own, e, got, g] + [x for _, x in groups] + [p, *q],
        [SMEM, SMEM] + [WHOLE] * (n + 5 + N),
        [HBM, WHOLE, HBM],
        vmem=24,
        scratch_shapes=[pltpu.VMEM((D, F), F32), pltpu.SemaphoreType.DMA((2 * N + 1,))],
    )


def later(array, behind):
    return lax.optimization_barrier((array, behind))[0]


def body(x, g, e, q_init):
    me = lax.axis_index("tensor")
    pos = jnp.stack([me % 2, lax.axis_index("dp")]).astype(jnp.int32)
    off = lax.dynamic_index_in_dim(jnp.asarray(block_tables()), me, 0, keepdims=False)
    e, q = pltpu.with_memory_space_constraint(e[0], pltpu.HBM), q_init.T

    mine, send = cut(pos, x)
    (x0,) = pack(stack_kernel, (mine, swap(send)), (2 * T,), ())
    a, b = hop(x0, True, 1), hop(x0, True, -1)
    g_other = swap(later(g, x0))
    own, other = tokens(off, q, g, (x0,))
    got = swap(other)
    g_other = held(g_other, (own,))
    h = add_parts(own, got, (g_other,))
    h = [h[0]] + [twin(v, False, bit) for v, bit in zip(h[1:], BITS[1:])]
    e_other = errors(pos, q, e, 1, (h[0],))
    top, bottom = pack(halves_kernel, (a, b), (T, T), (e_other, *h[1:]))
    c, d = hop(top, True, 1), hop(bottom, True, -1)

    (g0,) = pack(stack_kernel, (x0, a), (4 * T,), (top,))
    l0, r0 = hop(g0, False, 1), hop(g0, False, -1)
    e_got = swap(later(e_other, g0))
    e_own = errors(pos, q, e, 0, (g0,))
    (g1,) = pack(stack_kernel, (b, c, d), (4 * T,), (e_own, e_got))
    l1, r1 = hop(g1, False, 1), hop(g1, False, -1)

    keep, send = sketch_part(pos, h, (e_own, e_got), (g0, g1), ())
    got = hop_z(send, 1)
    near = [(0, g0), (4, g1)]
    acc = merge(off, pos, g, g_other, near, 0, H // 2, e, None, (send,))
    keep, send = add_pair(keep, got, (acc[0],))
    got = hop_z(send, 2)
    acc = merge(off, pos, g, g_other, near, H // 2, H, e, acc, (send,))
    (s,) = add([keep], [got], (acc[0],))
    got = twin(s, True, 1)
    l0, r0 = later(l0, s), later(r0, s)
    o0 = hop(l0, False, 1)
    mid = [(8, l0), (16, r0)]
    acc = merge(off, pos, g, g_other, mid, 0, H // 2, None, acc, (s,))
    (s,) = add([s], [got], (acc[0],))
    got = twin(s, True, 2)
    acc = merge(off, pos, g, g_other, mid, H // 2, H, None, acc, (s,))
    (s,) = add([s], [got], (acc[0],))
    s = swap(s)
    (s,) = add([s], [twin(s, True, 1)], ())
    (s,) = add([s], [twin(s, True, 2)], ())
    got = hop_z(s, 2)
    l1, r1 = later(l1, s), later(r1, s)
    o1 = hop(r1, False, -1)
    far = [(12, l1), (20, r1)]
    acc = merge(off, pos, g, g_other, far, 0, H // 2, None, acc, (s,))
    pair = jnp.stack([later(s, acc[0]), got])
    got = hop_z(pair, 1)
    acc = merge(off, pos, g, g_other, far, H // 2, H, None, acc, (pair,))
    stack = jnp.concatenate([later(pair, acc[0]), got])
    p = basis(pos, stack, swap(stack), (acc[0],))

    o0 = later(o0, p)
    qp, q_send, e_rest = right_part(pos, p, acc, e, ())
    qp, q_send = right_rest(off, pos, p, qp, q_send, g, g_other, [(24, o0)])
    o1 = later(o1, qp)
    last = [(24, o0), (28, o1)]
    qp, q_send = right_rest(off, pos, p, qp, q_send, g, g_other, last[1:])
    q_got = swap(q_send)
    out = last_other(off, acc[1], last, g_other, (q_send,))
    (qp,) = add([qp], [q_got], (out,))
    out = swap(later(out, qp))
    qs = (qp, around_z(qp, 2), around_z(qp, 1), around_z(qp, -1))
    err, qf, pf = final(off, pos, acc[0], e_rest, out, last, g, p, qs)
    return err[None], pf.T, qf.T


def solution(mesh):
    in_specs = (
        P(("dp", "tensor"), None),
        P("dp", "tensor"),
        P("dp", None, "tensor"),
        P("tensor", None),
    )
    out_specs = (P("dp", None, "tensor"), P(), P("tensor", None))
    return jax.shard_map(body, mesh=mesh, in_specs=in_specs, out_specs=out_specs, check_vma=False)
```
